32 devices in a mesh: dp: 16 (over z, y, x), tensor: 2 (over core).
Axes of the slice: x: 2, y: 2, z: 4, core: 2. Of those that a mesh axis runs over, the one named last changes fastest.
Arguments:
- tokens: bfloat16 [128, 185, 768], P('dp'), may hold values from -6 to 6
- cotangent: bfloat16 [128, 185, 768], P('dp'), may hold values from -6 to 6
- caption_lengths: int32 [128], P('dp'), may hold values from 5 to 40
- item_counts: int32 [16], P('dp'), may hold values from 1 to 8, as said below
- w_qkv: bfloat16 [768, 3, 768], P(None, None, 'tensor'), may hold values from -0.21875 to 0.21875
- qv_bias: float32 [2, 768], P(None, 'tensor'), may hold values from -2 to 2
- w_out: bfloat16 [768, 768], P('tensor'), may hold values from -0.625 to 0.625
- out_bias: float32 [768], replicated, may hold values from -2 to 2
- w_up: bfloat16 [768, 3072], P(None, 'tensor'), may hold values from -0.21875 to 0.21875
- up_bias: float32 [3072], P('tensor'), may hold values from -3 to 3
- w_down: bfloat16 [3072, 768], P('tensor'), may hold values from -0.109375 to 0.109375
- down_bias: float32 [768], replicated, may hold values from -2 to 2
- ln_gains: float32 [2, 768], replicated, may hold values from 0.5 to 1.5
- ln_biases: float32 [2, 768], replicated, may hold values from -2 to 2
Outputs:
- output: bfloat16 [128, 185, 768], P('dp')
- grad_tokens: bfloat16 [128, 185, 768], P('dp')
- grad_qkv: float32 [768, 3, 768], P(None, None, 'tensor')
- grad_qv_bias: float32 [2, 768], P(None, 'tensor')
- grad_out: float32 [768, 768], P('tensor')
- grad_out_bias: float32 [768], replicated
- grad_up: float32 [768, 3072], P(None, 'tensor')
- grad_up_bias: float32 [3072], P('tensor')
- grad_down: float32 [3072, 768], P('tensor')
- grad_down_bias: float32 [768], replicated
- grad_ln_gains: float32 [2, 768], replicated
- grad_ln_biases: float32 [2, 768], replicated
The draws below stay inside these ranges and needn't reach their ends.
Inputs may be any that keep to these rules, and one draw needn't show every extreme that they name: `item_counts`: item slots of a device at or beyond its count hold no item; some device has 8 live slots and some has 1.
All inputs are finite; a program needn't handle non-finite values.
Results may differ from the reference program's by a relative error of at most 0.013.
Values sent between devices are 32-bit elements; how exact they have to be, the bound alone decides.
No kernel may reach another device: no remote copies, remote signals or barrier semaphores. Data moves between devices by JAX's collectives and lax.ppermute only.
A program may use at most 192 MiB of HBM per device.

```python
import jax
import jax.numpy as jnp
from jax import lax

D = 768
HEADS = 12
HEAD_DIM = 64
FF = 3072
PATCHES = 144
CAPTION = 40
ITEMS_DEV = 8
SEQ = 185
ITEMS = 128
N_DP = 16


def draw_item_counts(key, part):
    key = jax.random.fold_in(key, 7)
    subkeys = jax.random.split(key, 3)
    counts = jax.random.randint(subkeys[0], (N_DP,), 1, ITEMS_DEV + 1)
    fullest = jax.random.randint(subkeys[1], (), 0, N_DP)
    lightest = (fullest + jax.random.randint(subkeys[2], (), 1, N_DP)) % N_DP
    counts = counts.at[fullest].set(ITEMS_DEV)
    counts = counts.at[lightest].set(1)
    return counts.astype(jnp.int32)


def with_ends(entries, rng, smallest, top_value):
    spot = [jax.random.randint(jax.random.fold_in(rng, axis), (), 0, length) for axis, length in enumerate(entries.shape)]
    main_axis = entries.shape.index(max(entries.shape))
    neighbour = spot[:main_axis] + [(spot[main_axis] + 1) % entries.shape[main_axis]] + spot[main_axis + 1:]
    return entries.at[tuple(spot)].set(smallest).at[tuple(neighbour)].set(top_value)


def levels(own_key, dims, cuts, least, top_value):
    loudness = 1.0
    for position, blocks in cuts:
        heights = jax.random.uniform(jax.random.fold_in(jax.random.fold_in(own_key, 6), position), (blocks,), jnp.float32, least / len(cuts), top_value / len(cuts))
        loudness = loudness * jnp.repeat(jnp.exp(heights), dims[position] // blocks).reshape((-1,) + (1,) * (len(dims) - 1 - position))
    return loudness


def normal_values(key, dims, scale, most, cuts=(), held_as=jnp.bfloat16):
    values = jax.random.normal(key, dims, jnp.float32) * scale
    if len(cuts) > 0:
        values = levels(key, dims, cuts, -0.22, 0.18) * values
    return jnp.clip(values, min=-most, max=most).astype(held_as)


def setup_inputs(seed: int = 0) -> dict:
    key_of = jax.random.split(jax.random.key(seed), 15)
    return {
        "tokens": normal_values(key_of[0], (ITEMS, SEQ, D), 1.0, 6.0, ((0, 16),)),
        "cotangent": normal_values(key_of[1], (ITEMS, SEQ, D), 1.0, 6.0, ((0, 16),)),
        "caption_lengths": with_ends(jax.random.randint(key_of[2], (ITEMS,), 5, CAPTION + 1), jax.random.fold_in(key_of[2], 1), 5, CAPTION).astype(jnp.int32),
        "item_counts": draw_item_counts(jax.random.fold_in(key_of[14], 71), 0),
        "w_qkv": normal_values(key_of[4], (D, 3, D), D ** -0.5, 0.21875, ((2, 2),)),
        "qv_bias": normal_values(key_of[5], (2, D), 0.3, 2.0, ((1, 2),), jnp.float32),
        "w_out": normal_values(key_of[6], (D, D), (D // 8) ** -0.5, 0.625, ((0, 2),)),
        "out_bias": normal_values(key_of[7], (D,), 0.3, 2.0, (), jnp.float32),
        "w_up": normal_values(key_of[8], (D, FF), D ** -0.5, 0.21875, ((1, 2),)),
        "up_bias": normal_values(key_of[9], (FF,), 0.5, 3.0, ((0, 2),), jnp.float32),
        "w_down": normal_values(key_of[10], (FF, D), FF ** -0.5, 0.109375, ((0, 2),)),
        "down_bias": normal_values(key_of[11], (D,), 0.3, 2.0, (), jnp.float32),
        "ln_gains": jnp.clip(1.0 + 0.1 * jax.random.normal(key_of[12], (2, D), jnp.float32), 0.5, 1.5),
        "ln_biases": normal_values(key_of[13], (2, D), 0.3, 2.0, (), jnp.float32),
    }


@jax.custom_vjp
def low(v):
    return lax.optimization_barrier(v.astype(jnp.bfloat16)).astype(jnp.float32)

@jax.custom_vjp
def low_back(v):
    return v

def low_keep(v):
    return (low(v), None)

def low_pass(kept, grad):
    return (grad,)

def back_keep(v):
    return (v, None)

def back_low(kept, grad):
    return (low(grad),)
low.defvjp(low_keep, low_pass)
low_back.defvjp(back_keep, back_low)
layer_eps = 1e-05

def precise(spec_text, left_side, right_side):
    return jnp.einsum(spec_text, left_side, right_side, precision=lax.Precision.HIGHEST)

def layer_norm(values, gain, shift):
    centred = values - lax.optimization_barrier(jnp.mean(values, axis=-1, keepdims=True))
    variance = lax.optimization_barrier(jnp.mean(centred * centred, axis=-1, keepdims=True))
    return centred * lax.rsqrt(variance + layer_eps) * gain + shift

def block_forward(params, inputs, key_valid):
    w_qkv, qv_bias, w_out, out_bias, w_up, up_bias, w_down, down_bias, ln_gains, ln_biases = params
    batch_items = inputs.shape[0]
    normed = low(layer_norm(inputs, ln_gains[0], ln_biases[0]))
    projected = precise('isd,dce->isce', normed, w_qkv)
    queries = low(low_back(projected[:, :, 0] + qv_bias[0]))
    keys_all = low(low_back(projected[:, :, 1]))
    values_all = low(low_back(projected[:, :, 2] + qv_bias[1]))
    heads_shape = (batch_items, SEQ, HEADS, HEAD_DIM)
    scores = precise('ishd,ithd->ihst', queries.reshape(heads_shape), keys_all.reshape(heads_shape))
    scores = low_back(scores * HEAD_DIM ** (-0.5))
    scores = jnp.where(key_valid[:, None, None, :], scores, -1e+30)
    soft_weights = low(jax.nn.softmax(scores, axis=-1))
    context = precise('ihst,ithd->ishd', soft_weights, values_all.reshape(heads_shape))
    context = low(low_back(context.reshape(batch_items, SEQ, D)))
    hidden = inputs + low_back(precise('isd,de->ise', context, w_out) + out_bias)
    second = low(layer_norm(hidden, ln_gains[1], ln_biases[1]))
    upward = low_back(precise('isd,df->isf', second, w_up) + up_bias)
    active = low(jax.nn.gelu(upward, approximate=False))
    return hidden + low_back(precise('isf,fd->isd', active, w_down) + down_bias)

def reference(tokens, cotangent, caption_lengths, item_counts, w_qkv, qv_bias, w_out, out_bias, w_up, up_bias, w_down, down_bias, ln_gains, ln_biases):
    params = jax.tree.map(lambda value: value.astype(jnp.float32), (w_qkv, qv_bias, w_out, out_bias, w_up, up_bias, w_down, down_bias, ln_gains, ln_biases))
    positions = jnp.arange(SEQ, dtype=jnp.int32)
    slot_ids = jnp.arange(ITEMS_DEV, dtype=jnp.int32)
    grouped = (tokens.reshape(N_DP, ITEMS_DEV, SEQ, D), cotangent.reshape(N_DP, ITEMS_DEV, SEQ, D), caption_lengths.reshape(N_DP, ITEMS_DEV).astype(jnp.int32), item_counts.astype(jnp.int32))

    def one_group(totals, group_data):
        inputs, upstream, lengths, live_count = group_data
        key_valid = positions[None, :] < PATCHES + 1 + lengths[:, None]
        live_mask = (slot_ids < live_count).astype(jnp.float32)[:, None, None]
        inputs = inputs.astype(jnp.float32)
        result, pullback = jax.vjp(lambda weights_in, feed_in: block_forward(weights_in, feed_in, key_valid), params, inputs)
        gradients, grad_inputs = pullback(upstream.astype(jnp.float32) * live_mask)
        totals = jax.tree.map(jnp.add, totals, gradients)
        return (totals, ((result * live_mask).astype(jnp.bfloat16), grad_inputs.astype(jnp.bfloat16)))
    zero_grads = jax.tree.map(jnp.zeros_like, params)
    totals, (outputs, grad_tokens) = lax.scan(one_group, zero_grads, grouped)
    return (outputs.reshape(ITEMS, SEQ, D), grad_tokens.reshape(ITEMS, SEQ, D), totals[0], totals[1], totals[2], totals[3], totals[4], totals[5], totals[6], totals[7], totals[8], totals[9])
```

```python
import jax
import jax.numpy as jnp
from jax import lax
from jax.experimental import pallas as pl
from jax.experimental.pallas import tpu as pltpu
from jax.sharding import PartitionSpec as P

HEAD_DIM = 64
PATCHES = 144
EPS = 1e-05
VMEM_LIMIT = 56 * 1024 * 1024
F32 = jnp.float32
BF16 = jnp.bfloat16


def mm(a, b, da=1, db=0):
    return lax.dot_general(a, b, (((da,), (db,)), ((), ())), preferred_element_type=F32)


def whole(shape):
    return pl.BlockSpec(shape, lambda *_: (0,) * len(shape))


def anywhere():
    return pl.BlockSpec(memory_space=pl.ANY)


def smem():
    return pl.BlockSpec(memory_space=pltpu.SMEM)


def call(body, grid, ins, in_specs, outs, out_specs, scratch=(), aliases=None, after=(), flops=0):
    n_in, n_after = len(ins), len(after)

    def kernel(*refs):
        body(*refs[:n_in], *refs[n_in + n_after :])

    size = sum(v.size * v.dtype.itemsize for v in ins) + sum(v.size * v.dtype.itemsize for v in outs)
    return pl.pallas_call(
        kernel,
        grid=grid,
        in_specs=list(in_specs) + [anywhere()] * n_after,
        out_specs=list(out_specs),
        out_shape=list(outs),
        scratch_shapes=list(scratch),
        input_output_aliases=aliases or {},
        compiler_params=pltpu.CompilerParams(vmem_limit_bytes=VMEM_LIMIT),
        cost_estimate=pl.CostEstimate(flops=int(flops), bytes_accessed=int(size), transcendentals=0),
    )(*ins, *after)


def sds(shape, dtype):
    return jax.ShapeDtypeStruct(shape, dtype)


def normed(v):
    centred = v - jnp.mean(v, axis=-1, keepdims=True)
    inverse = lax.rsqrt(jnp.mean(centred * centred, axis=-1, keepdims=True) + EPS)
    return centred * inverse, inverse


def norm_back(e, n, inverse, gain):
    eg = e * gain
    return inverse * (
        eg - jnp.mean(eg, axis=-1, keepdims=True) - n * jnp.mean(eg * n, axis=-1, keepdims=True)
    )


def colsum(v):
    return jnp.sum(v, axis=0, keepdims=True)


def on_device(
    tokens,
    cotangent,
    caption_lengths,
    item_counts,
    w_qkv,
    qv_bias,
    w_out,
    out_bias,
    w_up,
    up_bias,
    w_down,
    down_bias,
    ln_gains,
    ln_biases,
):
    items, seq, D = tokens.shape
    W = w_qkv.shape[2]
    FL = w_up.shape[1]
    pairs = W // 128
    heads = W // HEAD_DIM
    SP = -(-seq // 64) * 64
    R = items * SP
    IB = 2
    BR = IB * SP
    halves = 2
    steps = items // IB // halves
    total_steps = items // IB
    scale = HEAD_DIM ** (-0.5)

    wq = w_qkv.reshape(D, 3 * W)
    bias3 = jnp.concatenate([qv_bias[0], jnp.zeros((W,), F32), qv_bias[1]]).reshape(1, 3 * W)
    g1, g2 = ln_gains[0:1], ln_gains[1:2]
    b1, b2 = ln_biases[0:1], ln_biases[1:2]
    out_b = out_bias.reshape(1, D)
    down_b = down_bias.reshape(1, D)
    up_b = up_bias.reshape(1, FL)

    def padded(ref, i, scratch):
        rows = pl.ds(i * SP, seq)
        scratch[pl.ds(i * SP + seq // 8 * 8, SP - seq // 8 * 8), :] = jnp.zeros(
            (SP - seq // 8 * 8, D), F32
        )
        scratch[rows, :] = ref[i].astype(F32)

    def attn_fwd(off):
        def body(len_ref, tok_ref, wq_ref, b3_ref, g_ref, b_ref, wo_ref, *rest):
            part_ref, a_ref, qkv_ref, pr_ref, ctx_ref, xs = rest[-6:]
            step = pl.program_id(0)
            for i in range(IB):
                padded(tok_ref, i, xs)
            n, _ = normed(xs[...])
            a = (n * g_ref[...] + b_ref[...]).astype(BF16)
            a_ref[...] = a
            qkv_ref[...] = (mm(a, wq_ref[...]) + b3_ref[...]).astype(BF16)
            lane = lax.broadcasted_iota(jnp.int32, (SP, 128), 1)
            key_at = lax.broadcasted_iota(jnp.int32, (SP, SP), 0)
            zero = jnp.zeros((SP, 128), BF16)
            for i in range(IB):
                limit = PATCHES + 1 + len_ref[(step + off) * IB + i]
                valid = key_at < limit
                rows = pl.ds(i * SP, SP)
                for j in range(pairs):
                    q = qkv_ref[rows, pl.ds(j * 128, 128)] * jnp.asarray(scale, BF16)
                    k = qkv_ref[rows, pl.ds(W + j * 128, 128)]
                    v = qkv_ref[rows, pl.ds(2 * W + j * 128, 128)]
                    ctx = None
                    for s in range(2):
                        mine = (lane < 64) if s == 0 else (lane >= 64)
                        st = mm(k, jnp.where(mine, q, zero), 1, 1)
                        st = jnp.where(valid, st, -1e30)
                        e = jnp.exp(st - jnp.max(st, axis=0, keepdims=True))
                        pr = (e * (1.0 / jnp.sum(e, axis=0, keepdims=True))).astype(BF16)
                        pr_ref[i, 2 * j + s] = pr
                        c = mm(pr, jnp.where(mine, v, zero), 0, 0)
                        ctx = c if ctx is None else ctx + c
                    ctx_ref[rows, pl.ds(j * 128, 128)] = ctx.astype(BF16)
            part_ref[...] = mm(ctx_ref[...], wo_ref[...])

        return body

    kept = None
    parts = []
    for half in range(halves):
        off = half * steps
        row = lambda t, o=off: (t + o, 0)
        ins = [caption_lengths, tokens, wq, bias3, g1, b1, w_out]
        specs = [
            smem(),
            pl.BlockSpec((IB, seq, D), lambda t, o=off: (t + o, 0, 0)),
            whole((D, 3 * W)),
            whole((1, 3 * W)),
            whole((1, D)),
            whole((1, D)),
            whole((W, D)),
        ]
        outs = [
            sds((R // halves, D), F32),
            sds((R, D), BF16),
            sds((R, 3 * W), BF16),
            sds((items, heads, SP, SP), BF16),
            sds((R, W), BF16),
        ]
        out_specs = [
            pl.BlockSpec((BR, D), lambda t: (t, 0)),
            pl.BlockSpec((BR, D), row),
            pl.BlockSpec((BR, 3 * W), row),
            pl.BlockSpec((IB, heads, SP, SP), lambda t, o=off: (t + o, 0, 0, 0)),
            pl.BlockSpec((BR, W), row),
        ]
        aliases = {}
        if kept is not None:
            aliases = {len(ins) + n: 1 + n for n in range(4)}
            ins += kept
            specs += [anywhere()] * 4
        res = call(
            attn_fwd(off),
            (steps,),
            ins,
            specs,
            outs,
            out_specs,
            [pltpu.VMEM((BR, D), F32)],
            aliases,
            flops=R * D * W * 4,
        )
        parts.append(res[0])
        kept = list(res[1:])
    a_all, qkv, prs, ctx_all = kept

    swap = [(0, 1), (1, 0)]

    def other(v):
        return lax.ppermute(v, "tensor", swap)

    got = [other(p) for p in parts]

    def second(off):
        def body(cnt_ref, tok_ref, cot_ref, p_ref, r_ref, ob_ref, g_ref, b_ref, *rest):
            h_ref, c_ref, ct_ref, dy_ref, sum_ref, xs = rest[-6:]
            step = pl.program_id(0)
            for i in range(IB):
                padded(tok_ref, i, xs)
            h = xs[...] + (p_ref[...] + r_ref[...]) + ob_ref[...]
            h_ref[...] = h.astype(BF16)
            n, _ = normed(h)
            c = (n * g_ref[...] + b_ref[...]).astype(BF16)
            c_ref[...] = c
            ct_ref[...] = c.T
            for i in range(IB):
                padded(cot_ref, i, xs)
            item = (step + off) * IB + lax.broadcasted_iota(jnp.int32, (BR, D), 0) // SP
            dy = jnp.where(item < cnt_ref[0], xs[...], 0.0)
            dy_ref[...] = dy.astype(BF16)
            sum_ref[0] = colsum(dy)

        return body

    kept = None
    for half in range(halves):
        off = half * steps
        row = lambda t, o=off: (t + o, 0)
        tok_spec = pl.BlockSpec((IB, seq, D), lambda t, o=off: (t + o, 0, 0))
        ins = [item_counts, tokens, cotangent, parts[half], got[half], out_b, g2, b2]
        specs = [
            smem(),
            tok_spec,
            tok_spec,
            pl.BlockSpec((BR, D), lambda t: (t, 0)),
            pl.BlockSpec((BR, D), lambda t: (t, 0)),
            whole((1, D)),
            whole((1, D)),
            whole((1, D)),
        ]
        outs = [
            sds((R, D), BF16),
            sds((R, D), BF16),
            sds((D, R), BF16),
            sds((R, D), BF16),
            sds((total_steps, 1, D), F32),
        ]
        out_specs = [
            pl.BlockSpec((BR, D), row),
            pl.BlockSpec((BR, D), row),
            pl.BlockSpec((D, BR), lambda t, o=off: (0, t + o)),
            pl.BlockSpec((BR, D), row),
            pl.BlockSpec((1, 1, D), lambda t, o=off: (t + o, 0, 0)),
        ]
        aliases = {}
        if kept is not None:
            aliases = {len(ins) + n: n for n in range(5)}
            ins += kept
            specs += [anywhere()] * 5
        kept = list(
            call(second(off), (steps,), ins, specs, outs, out_specs, [pltpu.VMEM((BR, D), F32)], aliases)
        )
    h_all, c_all, ct_all, dy_all, dy_sums = kept

    FC = 384 if FL % 384 == 0 else FL
    RB = R // 2
    SB = 256

    def ffn(f):
        def body(c_ref, ct_ref, dy_ref, wu_ref, ub_ref, wd_ref, *rest):
            gd_ref, gu_ref, sum_ref, r_ref, du_ref = rest[-5:]
            step = pl.program_id(0)
            total = None
            for s in range(RB // SB):
                rows = pl.ds(s * SB, SB)
                u = mm(c_ref[rows, :], wu_ref[...]) + ub_ref[...]
                half_erf = 0.5 + 0.5 * lax.erf(u * (0.5**0.5))
                r_ref[rows, :] = (u * half_erf).astype(BF16)
                slope = half_erf + u * (jnp.exp(-0.5 * u * u) * 0.3989422804014327)
                dr = mm(dy_ref[rows, :], wd_ref[...], 1, 1)
                du = (dr * slope).astype(BF16)
                du_ref[rows, :] = du
                t = colsum(du.astype(F32))
                total = t if total is None else total + t
            gd = mm(r_ref[...], dy_ref[...], 0, 0)
            gu = mm(ct_ref[...], du_ref[...])

            @pl.when(step == 0)
            def _():
                gd_ref[...] = gd
                gu_ref[...] = gu
                sum_ref[...] = total

            @pl.when(step > 0)
            def _():
                gd_ref[...] += gd
                gu_ref[...] += gu
                sum_ref[...] += total

        return body

    kept = None
    gds, gus, up_sums = [], [], []
    for f in range(FL // FC):
        ins = [c_all, ct_all, dy_all, w_up, up_b, w_down]
        specs = [
            pl.BlockSpec((RB, D), lambda t: (t, 0)),
            pl.BlockSpec((D, RB), lambda t: (0, t)),
            pl.BlockSpec((RB, D), lambda t: (t, 0)),
            pl.BlockSpec((D, FC), lambda t, f=f: (0, f)),
            pl.BlockSpec((1, FC), lambda t, f=f: (0, f)),
            pl.BlockSpec((FC, D), lambda t, f=f: (f, 0)),
        ]
        outs = [
            sds((FC, D), F32),
            sds((D, FC), F32),
            sds((1, FC), F32),
            sds((R, FL), BF16),
            sds((R, FL), BF16),
        ]
        out_specs = [
            whole((FC, D)),
            whole((D, FC)),
            whole((1, FC)),
            pl.BlockSpec((RB, FC), lambda t, f=f: (t, f)),
            pl.BlockSpec((RB, FC), lambda t, f=f: (t, f)),
        ]
        aliases = {}
        if kept is not None:
            aliases = {len(ins) + n: 3 + n for n in range(2)}
            ins += kept
            specs += [anywhere()] * 2
        gd, gu, us, r_all, du_all = call(
            ffn(f), (R // RB,), ins, specs, outs, out_specs, (), aliases, flops=8 * R * D * FC
        )
        kept = [r_all, du_all]
        gds.append(gd)
        gus.append(gu)
        up_sums.append(us)

    def dc_body(du_ref, w_ref, o_ref):
        o_ref[...] = mm(du_ref[...], w_ref[...], 1, 1)

    def y_body(r_ref, w_ref, o_ref):
        o_ref[...] = mm(r_ref[...], w_ref[...])

    MB = R // 4
    (dc_part,) = call(
        dc_body,
        (R // MB,),
        [du_all, w_up],
        [pl.BlockSpec((MB, FL), lambda t: (t, 0)), whole((D, FL))],
        [sds((R, D), F32)],
        [pl.BlockSpec((MB, D), lambda t: (t, 0))],
        flops=2 * R * D * FL,
    )
    dc_got = other(dc_part)
    (y_part,) = call(
        y_body,
        (R // MB,),
        [r_all, w_down],
        [pl.BlockSpec((MB, FL), lambda t: (t, 0)), whole((FL, D))],
        [sds((R, D), F32)],
        [pl.BlockSpec((MB, D), lambda t: (t, 0))],
        flops=2 * R * D * FL,
        after=(dc_part,),
    )
    y_got = other(y_part)

    def back2_body(p_ref, r_ref, h_ref, dy_ref, ctx_ref, wo_ref, g_ref, dh_ref, dctx_ref, go_ref, sum_ref):
        step = pl.program_id(0)
        e = p_ref[...] + r_ref[...]
        n, inverse = normed(h_ref[...].astype(F32))
        dh = dy_ref[...].astype(F32) + norm_back(e, n, inverse, g_ref[...])
        dhr = dh.astype(BF16)
        dh_ref[...] = dhr
        dctx_ref[...] = mm(dhr, wo_ref[...], 1, 1).astype(BF16)
        sum_ref[0, 0:1] = colsum(e * n)
        sum_ref[0, 1:2] = colsum(e)
        sum_ref[0, 2:3] = colsum(dhr.astype(F32))
        go = mm(ctx_ref[...], dhr, 0, 0)

        @pl.when(step == 0)
        def _():
            go_ref[...] = go

        @pl.when(step > 0)
        def _():
            go_ref[...] += go

    rowD = pl.BlockSpec((BR, D), lambda t: (t, 0))
    rowW = pl.BlockSpec((BR, W), lambda t: (t, 0))
    row3 = pl.BlockSpec((BR, 3 * W), lambda t: (t, 0))
    dh_all, dctx_all, go, back2_sums = call(
        back2_body,
        (total_steps,),
        [dc_part, dc_got, h_all, dy_all, ctx_all, w_out, g2],
        [rowD, rowD, rowD, rowD, rowW, whole((W, D)), whole((1, D))],
        [sds((R, D), BF16), sds((R, W), BF16), sds((W, D), F32), sds((total_steps, 3, D), F32)],
        [rowD, rowW, whole((W, D)), pl.BlockSpec((1, 3, D), lambda t: (t, 0, 0))],
        after=(y_part,),
        flops=4 * R * D * W,
    )

    def attn_back_body(pr_ref, qkv_ref, dctx_ref, wq_ref, dqkv_ref, da_ref, sum_ref):
        lane = lax.broadcasted_iota(jnp.int32, (SP, 128), 1)
        zero = jnp.zeros((SP, 128), BF16)
        for i in range(IB):
            rows = pl.ds(i * SP, SP)
            for j in range(pairs):
                q = qkv_ref[rows, pl.ds(j * 128, 128)] * jnp.asarray(scale, BF16)
                k = qkv_ref[rows, pl.ds(W + j * 128, 128)]
                v = qkv_ref[rows, pl.ds(2 * W + j * 128, 128)]
                dctx = dctx_ref[rows, pl.ds(j * 128, 128)]
                dq = dk = dv = None
                for s in range(2):
                    mine = (lane < 64) if s == 0 else (lane >= 64)
                    pr = pr_ref[i, 2 * j + s]
                    dc = jnp.where(mine, dctx, zero)
                    dv_h = mm(pr, dc)
                    dp = mm(v, dc, 1, 1)
                    p = pr.astype(F32)
                    pdp = p * dp
                    ds = (pdp - p * jnp.sum(pdp, axis=0, keepdims=True)).astype(BF16)
                    dk_h = mm(ds, jnp.where(mine, q, zero))
                    dq_h = mm(ds, jnp.where(mine, k, zero), 0, 0)
                    dq = dq_h if dq is None else dq + dq_h
                    dk = dk_h if dk is None else dk + dk_h
                    dv = dv_h if dv is None else dv + dv_h
                dqkv_ref[rows, pl.ds(j * 128, 128)] = (dq * scale).astype(BF16)
                dqkv_ref[rows, pl.ds(W + j * 128, 128)] = dk.astype(BF16)
                dqkv_ref[rows, pl.ds(2 * W + j * 128, 128)] = dv.astype(BF16)
        dqkv = dqkv_ref[...]
        da_ref[...] = mm(dqkv, wq_ref[...], 1, 1)
        sum_ref[0] = colsum(dqkv.astype(F32))

    dqkv, da_part, qkv_sums = call(
        attn_back_body,
        (total_steps,),
        [prs, qkv, dctx_all, wq],
        [
            pl.BlockSpec((IB, heads, SP, SP), lambda t: (t, 0, 0, 0)),
            row3,
            rowW,
            whole((D, 3 * W)),
        ],
        [sds((R, 3 * W), BF16), sds((R, D), F32), sds((total_steps, 1, 3 * W), F32)],
        [row3, rowD, pl.BlockSpec((1, 1, 3 * W), lambda t: (t, 0, 0))],
        flops=6 * R * D * W,
    )
    da_got = other(da_part)

    def gqkv_body(a_ref, dqkv_ref, o_ref, at):
        @pl.when(pl.program_id(0) == 0)
        def _():
            at[...] = a_ref[...].T

        o_ref[0] = mm(at[...], dqkv_ref[...])

    (gqkv,) = call(
        gqkv_body,
        (3,),
        [a_all, dqkv],
        [whole((R, D)), pl.BlockSpec((R, W), lambda t: (0, t))],
        [sds((3, D, W), F32)],
        [pl.BlockSpec((1, D, W), lambda t: (t, 0, 0))],
        [pltpu.VMEM((D, R), BF16)],
        flops=6 * R * D * W,
        after=(da_part,),
    )

    def back1_body(tok_ref, p_ref, r_ref, dh_ref, g_ref, o_ref, sum_ref, xs):
        for i in range(IB):
            padded(tok_ref, i, xs)
        e = p_ref[...] + r_ref[...]
        n, inverse = normed(xs[...])
        dx = dh_ref[...].astype(F32) + norm_back(e, n, inverse, g_ref[...])
        xs[...] = dx
        for i in range(IB):
            o_ref[i] = xs[pl.ds(i * SP, seq), :].astype(BF16)
        sum_ref[0, 0:1] = colsum(e * n)
        sum_ref[0, 1:2] = colsum(e)

    tok_spec = pl.BlockSpec((IB, seq, D), lambda t: (t, 0, 0))
    grad_tokens, back1_sums = call(
        back1_body,
        (total_steps,),
        [tokens, da_part, da_got, dh_all, g1],
        [tok_spec, rowD, rowD, rowD, whole((1, D))],
        [sds(tokens.shape, BF16), sds((total_steps, 2, D), F32)],
        [tok_spec, pl.BlockSpec((1, 2, D), lambda t: (t, 0, 0))],
        [pltpu.VMEM((BR, D), F32)],
        after=(gqkv,),
    )

    def out_body(cnt_ref, h_ref, p_ref, r_ref, b_ref, o_ref, xs):
        step = pl.program_id(0)
        y = h_ref[...].astype(F32) + (p_ref[...] + r_ref[...]) + b_ref[...]
        item = step * IB + lax.broadcasted_iota(jnp.int32, (BR, D), 0) // SP
        xs[...] = jnp.where(item < cnt_ref[0], y, 0.0)
        for i in range(IB):
            o_ref[i] = xs[pl.ds(i * SP, seq), :].astype(BF16)

    (output,) = call(
        out_body,
        (total_steps,),
        [item_counts, h_all, y_part, y_got, down_b],
        [smem(), rowD, rowD, rowD, whole((1, D))],
        [sds(tokens.shape, BF16)],
        [tok_spec],
        [pltpu.VMEM((BR, D), F32)],
        after=(grad_tokens,),
    )

    small = jnp.concatenate(
        [
            jnp.sum(qkv_sums, axis=(0, 1))[: W],
            jnp.sum(qkv_sums, axis=(0, 1))[2 * W :],
            jnp.sum(back2_sums, axis=0).reshape(-1),
            jnp.concatenate([s.reshape(-1) for s in up_sums]),
            jnp.sum(dy_sums, axis=(0, 1)),
            jnp.sum(back1_sums, axis=0).reshape(-1),
        ]
    )
    gds, gus = lax.psum((gds, gus), "dp")
    gqkv, go, small = lax.psum((gqkv, go, small), "dp")
    grad_down = jnp.concatenate(gds, axis=0)
    grad_up = jnp.concatenate(gus, axis=1)
    grad_qkv = jnp.transpose(gqkv, (1, 0, 2))
    at = 0

    def take(n):
        nonlocal at
        at += n
        return small[at - n : at]

    grad_qv_bias = take(2 * W).reshape(2, W)
    gain2, shift2, grad_out_bias = take(D), take(D), take(D)
    grad_up_bias = take(FL)
    grad_down_bias = take(D)
    gain1, shift1 = take(D), take(D)
    return (
        output,
        grad_tokens,
        grad_qkv,
        grad_qv_bias,
        go,
        grad_out_bias,
        grad_up,
        grad_up_bias,
        grad_down,
        grad_down_bias,
        jnp.stack([gain1, gain2]),
        jnp.stack([shift1, shift2]),
    )


def solution(mesh):
    return jax.shard_map(
        on_device,
        mesh=mesh,
        in_specs=(
            P("dp", None, None),
            P("dp", None, None),
            P("dp"),
            P("dp"),
            P(None, None, "tensor"),
            P(None, "tensor"),
            P("tensor", None),
            P(),
            P(None, "tensor"),
            P("tensor"),
            P("tensor", None),
            P(),
            P(),
            P(),
        ),
        out_specs=(
            P("dp", None, None),
            P("dp", None, None),
            P(None, None, "tensor"),
            P(None, "tensor"),
            P("tensor", None),
            P(),
            P(None, "tensor"),
            P("tensor"),
            P("tensor", None),
            P(),
            P(),
            P(),
        ),
        check_vma=False,
    )
```

```python
import jax
import jax.numpy as jnp
from jax import lax
from jax.experimental import pallas as pl
from jax.experimental.pallas import tpu as pltpu
from jax.sharding import PartitionSpec as P

HEAD_DIM = 64
PATCHES = 144
EPS = 1e-05
MIB = 1024 * 1024
COST = 1024
F32 = jnp.float32
BF16 = jnp.bfloat16


def mm(a, b, da=1, db=0):
    return lax.dot_general(a, b, (((da,), (db,)), ((), ())), preferred_element_type=F32)


def whole(shape):
    return pl.BlockSpec(shape, lambda *_: (0,) * len(shape))


def anywhere():
    return pl.BlockSpec(memory_space=pl.ANY)


def smem():
    return pl.BlockSpec(memory_space=pltpu.SMEM)


def in_hbm(v):
    return pltpu.with_memory_space_constraint(v, pltpu.HBM)


def here(v):
    return pltpu.with_memory_space_constraint(v, pltpu.VMEM)


class Order:
    def __init__(self):
        self.last = ()


def call(body, grid, ins, in_specs, outs, out_specs, scratch=(), aliases=None, order=None, vmem=24):
    n_in, n_out = len(ins), len(outs)

    def kernel(*refs):
        after_in = n_in + len(order.last)
        body(*refs[:n_in], *refs[after_in : after_in + n_out], *refs[after_in + n_out + 1 :])

    *res, token = pl.pallas_call(
        kernel,
        grid=grid,
        in_specs=list(in_specs) + [anywhere()] * len(order.last),
        out_specs=list(out_specs) + [anywhere()],
        out_shape=list(outs) + [pltpu.HBM((8, 128), F32)],
        scratch_shapes=list(scratch),
        input_output_aliases=aliases or {},
        compiler_params=pltpu.CompilerParams(vmem_limit_bytes=vmem * MIB),
        cost_estimate=pl.CostEstimate(flops=COST, bytes_accessed=COST, transcendentals=0),
    )(*ins, *[in_hbm(v) for v in order.last])
    order.last = (token,)
    return res


def sds(shape, dtype):
    return jax.ShapeDtypeStruct(shape, dtype)


def normed(v):
    centred = v - jnp.mean(v, axis=-1, keepdims=True)
    inverse = lax.rsqrt(jnp.mean(centred * centred, axis=-1, keepdims=True) + EPS)
    return centred * inverse, inverse


def norm_back(e, n, inverse, gain):
    eg = e * gain
    return inverse * (
        eg - jnp.mean(eg, axis=-1, keepdims=True) - n * jnp.mean(eg * n, axis=-1, keepdims=True)
    )


def colsum(v):
    return jnp.sum(v, axis=0, keepdims=True)


def in_vmem():
    return pl.BlockSpec(memory_space=pltpu.VMEM)


BITS = {"x": 0, "y": 1, "a": 2, "b": 3}


hbm = pltpu.HBM
vmem = pltpu.VMEM


class Links:
    def __init__(self, n_dp, n_t):
        self.n_dp, self.n_t = n_dp, n_t
        self.extra = tuple(range(4, n_dp.bit_length() - 1))

    def swap(self, v, dims):
        pairs = [
            (d * self.n_t + t, (d ^ (1 << BITS.get(dims[t % 2], dims[t % 2]))) * self.n_t + t)
            for d in range(self.n_dp)
            for t in range(self.n_t)
        ]
        return lax.ppermute(v, ("dp", "tensor"), pairs)

    def bit(self, dims):
        d, t = lax.axis_index("dp"), lax.axis_index("tensor") % 2
        return (d >> jnp.where(t == 0, BITS[dims[0]], BITS[dims[1]])) & 1


def add_split(keep, got, bit, order):
    n, width = keep.shape
    h = n // 2

    def body(b_ref, k_ref, r_ref, ko_ref, so_ref):
        mine = pl.ds(pl.multiple_of(b_ref[0] * h, 8), h)
        rest = pl.ds(pl.multiple_of((1 - b_ref[0]) * h, 8), h)
        so_ref[...] = k_ref[rest, :] + r_ref[rest, :]
        ko_ref[...] = k_ref[mine, :] + r_ref[mine, :]

    return call(
        body, (), [bit.reshape(1), keep, got], [smem(), in_vmem(), in_vmem()],
        [sds((h, width), F32)] * 2, [in_vmem()] * 2, order=order, vmem=8,
    )


def add(keep, got, order):
    def body(k_ref, r_ref, o_ref):
        o_ref[...] = k_ref[...] + r_ref[...]

    return call(
        body, (), [keep, got], [in_vmem()] * 2, [sds(keep.shape, F32)], [in_vmem()], order=order, vmem=8
    )[0]


def join(mine, got, bit, order):
    n, width = mine.shape

    def body(b_ref, m_ref, r_ref, o_ref):
        o_ref[pl.ds(pl.multiple_of(b_ref[0] * n, 8), n), :] = m_ref[...]
        o_ref[pl.ds(pl.multiple_of((1 - b_ref[0]) * n, 8), n), :] = r_ref[...]

    return call(
        body, (), [bit.reshape(1), mine, got], [smem(), in_vmem(), in_vmem()],
        [sds((2 * n, width), F32)], [in_vmem()], order=order, vmem=8,
    )[0]


class Piece:
    def __init__(self, links, dims, keep, send, finish):
        self.links, self.finish = links, finish
        halving = list(zip(*dims))
        whole = [("b", "b")] + [(e, e) for e in links.extra]
        self.stages = (
            [(d, "half") for d in halving] + [(d, "whole") for d in whole] + [(d, "back") for d in halving[::-1]]
        )
        self.at = 0
        self.keep = keep
        self.got = links.swap(send, halving[0])

    def step(self, order):
        dim, kind = self.stages[self.at]
        self.at += 1
        if self.at == len(self.stages):
            self.finish(self.keep, self.got, order)
            return
        following, next_kind = self.stages[self.at]
        if kind == "back":
            self.keep = send = join(self.keep, self.got, self.links.bit(dim), order)
        elif next_kind == "half":
            self.keep, send = add_split(self.keep, self.got, self.links.bit(following), order)
        else:
            self.keep = send = add(self.keep, self.got, order)
        self.got = self.links.swap(send, following)


def on_device(
    links,
    plan,
    tokens,
    cotangent,
    caption_lengths,
    item_counts,
    w_qkv,
    qv_bias,
    w_out,
    out_bias,
    w_up,
    up_bias,
    w_down,
    down_bias,
    ln_gains,
    ln_biases,
):
    order = Order()
    first_bit = [links.bit((v[0][0], v[1][0])).reshape(1) for v in plan["dims"]]
    items, seq, D = tokens.shape
    W = w_qkv.shape[2]
    FL = w_up.shape[1]
    pairs = W // 128
    heads = W // HEAD_DIM
    SP = -(-seq // 64) * 64
    R = items * SP
    IB = 2
    BR = IB * SP
    steps = items // IB
    scale = HEAD_DIM ** (-0.5)

    wq = jnp.transpose(w_qkv, (1, 0, 2))
    bias3 = jnp.concatenate([qv_bias[0], jnp.zeros((W,), F32), qv_bias[1]]).reshape(1, 3 * W)
    g1, g2 = ln_gains[0:1], ln_gains[1:2]
    b1, b2 = ln_biases[0:1], ln_biases[1:2]
    out_b = out_bias.reshape(1, D)
    down_b = down_bias.reshape(1, D)
    up_b = up_bias.reshape(1, FL)
    by_token = (1, 0, 2)
    state = {}
    pieces = {}
    up_sums = []
    swap = [(0, 1), (1, 0)]

    def other(v):
        return lax.ppermute(v, "tensor", swap)

    rowD = pl.BlockSpec((BR, D), lambda t: (t, 0))
    rowW = pl.BlockSpec((BR, W), lambda t: (t, 0))
    row3 = pl.BlockSpec((BR, 3 * W), lambda t: (t, 0))

    def release(arrays, space):
        n = len(arrays)
        return call(
            lambda *refs: None,
            (),
            [pltpu.with_memory_space_constraint(v, space) for v in arrays],
            [anywhere()] * n,
            [space(v.shape, v.dtype) for v in arrays],
            [anywhere()] * n,
            aliases={i: i for i in range(n)},
            order=order,
            vmem=4,
        )

    def dc_send():
        state["dc"] = release([state["dc"]], vmem)[0]
        state["dc_got"] = other(state["dc"])

    def da_send():
        state["da"] = release([state["da"]], vmem)[0]
        state["da_got"] = other(state["da"])

    def y_send():
        state["y"] = release([state["y"]], hbm)[0]
        state["y_got"] = other(state["y"])

    def spread(name, source, masked):
        def body(cnt_ref, t_ref, o_ref, sum_ref, xs):
            for k in range(D // 128):
                cols = pl.ds(k * 128, 128)
                xs[k, pl.ds(seq * items, (SP - seq) * items), :] = jnp.zeros(((SP - seq) * items, 128), F32)
                xs[k, pl.ds(0, seq * items), :] = t_ref[:, :, cols].astype(F32).reshape(seq * items, 128)
                total = jnp.zeros((1, 128), F32)
                for i in range(items):
                    v = xs[k, pl.ds(i, SP, stride=items), :]
                    if masked:
                        v = jnp.where(i < cnt_ref[0], v, 0.0)
                        total = total + colsum(v)
                    o_ref[pl.ds(i * SP, SP), cols] = v.astype(BF16)
                sum_ref[:, cols] = total

        state[name], state[name + "_sum"] = call(
            body,
            (),
            [item_counts, jnp.transpose(source, by_token)],
            [smem(), in_vmem()],
            [vmem((R, D), BF16), sds((1, D), F32)],
            [in_vmem(), in_vmem()],
            [pltpu.VMEM((D // 128, SP * items, 128), F32)],
            order=order,
        )

    def attn_fwd(half):
        def body(len_ref, x_ref, wq_ref, b3_ref, g_ref, b_ref, wo_ref, *rest):
            part_ref, a_ref, qkv_ref, pr_ref, ctx_ref, kept_ref = rest[-6:]
            step = pl.program_id(0)
            kept_ref[...] = x_ref[...]
            n, _ = normed(x_ref[...].astype(F32))
            a = (n * g_ref[...] + b_ref[...]).astype(BF16)
            a_ref[...] = a
            for c in range(3):
                cols = pl.ds(c * W, W)
                qkv_ref[:, cols] = (mm(a, wq_ref[c]) + b3_ref[:, cols]).astype(BF16)
            lane = lax.broadcasted_iota(jnp.int32, (SP, 128), 1)
            key_at = lax.broadcasted_iota(jnp.int32, (SP, SP), 0)
            zero = jnp.zeros((SP, 128), BF16)
            for i in range(IB):
                limit = PATCHES + 1 + len_ref[(step + half * (steps // 2)) * IB + i]
                valid = key_at < limit
                rows = pl.ds(i * SP, SP)
                for j in range(pairs):
                    q = qkv_ref[rows, pl.ds(j * 128, 128)] * jnp.asarray(scale, BF16)
                    k = qkv_ref[rows, pl.ds(W + j * 128, 128)]
                    v = qkv_ref[rows, pl.ds(2 * W + j * 128, 128)]
                    ctx = None
                    for s in range(2):
                        mine = (lane < 64) if s == 0 else (lane >= 64)
                        st = mm(k, jnp.where(mine, q, zero), 1, 1)
                        st = jnp.where(valid, st, -1e30)
                        e = jnp.exp(st - jnp.max(st, axis=0, keepdims=True))
                        pr = (e * (1.0 / jnp.sum(e, axis=0, keepdims=True))).astype(BF16)
                        pr_ref[i, 2 * j + s] = pr
                        c = mm(pr, jnp.where(mine, v, zero), 0, 0)
                        ctx = c if ctx is None else ctx + c
                    ctx_ref[rows, pl.ds(j * 128, 128)] = ctx.astype(BF16)
            part_ref[...] = mm(ctx_ref[...], wo_ref[...])

        off = half * (steps // 2)
        row = lambda t: (t + off, 0)
        ins = [caption_lengths, state["x"], wq, bias3, g1, b1, w_out]
        specs = [
            smem(),
            pl.BlockSpec((BR, D), row),
            in_vmem(),
            in_vmem(),
            in_vmem(),
            in_vmem(),
            in_vmem(),
        ]
        outs = [
            vmem((R // 2, D), F32),
            hbm((R, D), BF16),
            hbm((R, 3 * W), BF16),
            hbm((items, heads, SP, SP), BF16),
            hbm((R, W), BF16),
            hbm((R, D), BF16),
        ]
        out_specs = [
            rowD,
            pl.BlockSpec((BR, D), row),
            pl.BlockSpec((BR, 3 * W), row),
            pl.BlockSpec((IB, heads, SP, SP), lambda t: (t + off, 0, 0, 0)),
            pl.BlockSpec((BR, W), row),
            pl.BlockSpec((BR, D), row),
        ]
        names = ("a", "qkv", "pr", "ctx", "x_kept")
        aliases = {}
        if half:
            aliases = {len(ins) + n: 1 + n for n in range(5)}
            ins += [in_hbm(state[v]) for v in names]
            specs += [anywhere()] * 5
        part, *kept = call(
            body, (steps // 2,), ins, specs, outs, out_specs, (), aliases, order=order
        )
        state.update(zip(names, kept))
        return part

    spread("x", tokens, False)
    parts, got = [], []
    for half in range(2):
        part = attn_fwd(half)
        parts.append(part)
        got.append(other(part))
        if half == 0:
            spread("dy", cotangent, True)

    def second(half):
        def body(x_ref, p_ref, r_ref, ob_ref, g_ref, b_ref, *rest):
            h_ref, c_ref, ct_ref = rest[-3:]
            h = x_ref[...].astype(F32) + (p_ref[...] + r_ref[...]) + ob_ref[...]
            h_ref[...] = h.astype(BF16)
            n, _ = normed(h)
            c = (n * g_ref[...] + b_ref[...]).astype(BF16)
            c_ref[...] = c
            ct_ref[...] = c.T

        off = half * (steps // 2)
        row = lambda t: (t + off, 0)
        ins = [state["x"], parts[half], got[half], out_b, g2, b2]
        specs = [pl.BlockSpec((BR, D), row), rowD, rowD, in_vmem(), in_vmem(), in_vmem()]
        outs = [hbm((R, D), BF16), vmem((R, D), BF16), vmem((D, R), BF16)]
        out_specs = [
            pl.BlockSpec((BR, D), row),
            pl.BlockSpec((BR, D), row),
            pl.BlockSpec((D, BR), lambda t: (0, t + off)),
        ]
        names = ("h", "c", "ct")
        aliases = {}
        if half:
            aliases = {len(ins) + n: n for n in range(3)}
            ins += [in_hbm(state["h"]), here(state["c"]), here(state["ct"])]
            specs += [anywhere()] * 3
        kept = call(
            body, (steps // 2,), ins, specs, outs, out_specs, (), aliases, order=order
        )
        state.update(zip(names, kept))

    second(0)
    second(1)

    HU = 256
    FC = 2 * HU
    chunks = FL // FC
    SB = 256
    DH = D // 2
    lanes = D // HU

    def ffn(f):
        def body(p_ref, c_ref, ct_ref, dy_ref, wu_ref, ub_ref, wd_ref, keep_ref, send_ref, sum_ref, r_out, du_out, *rest):
            r_ref, du_ref, acc, sems = rest
            p = p_ref[0]
            units = [pl.ds((f + side * chunks) * HU, HU) for side in range(2)]
            copies = []

            def copy_out(source, target):
                copy = pltpu.make_async_copy(source, target, sems.at[len(copies)])
                copy.start()
                copies.append(copy)

            totals = [jnp.zeros((1, HU), F32)] * 2
            for s in range(R // SB):
                rows = pl.ds(s * SB, SB)
                c = c_ref[rows, :]
                dy = dy_ref[rows, :]
                for side in range(2):
                    cols = pl.ds(side * HU, HU)
                    u = mm(c, wu_ref[:, units[side]]) + ub_ref[:, units[side]]
                    dr = mm(dy, wd_ref[units[side], :], 1, 1)
                    below = 0.5 + 0.5 * lax.erf(u * (0.5**0.5))
                    density = jnp.exp(-0.5 * u * u) * 0.3989422804014327
                    r_ref[rows, cols] = (u * below).astype(BF16)
                    du = (dr * (below + u * density)).astype(BF16)
                    du_ref[rows, cols] = du
                    totals[side] = totals[side] + colsum(du.astype(F32))
            for side in range(2):
                sum_ref[:, pl.ds(side * HU, HU)] = totals[side]
            copy_out(r_ref, r_out)
            copy_out(du_ref, du_out)
            gd = mm(r_ref[...], dy_ref[...], 0, 0)
            for half in range(2):
                acc[half, pl.ds(0, HU), :] = gd[half * HU : (half + 1) * HU]
            copy_out(acc.at[1 - p, pl.ds(0, HU)], send_ref.at[pl.ds(0, HU)])
            gu = mm(ct_ref[...], du_ref[...])
            for half in range(2):
                for j in range(HU // 128):
                    for b in range(lanes):
                        for side in range(2):
                            acc[half, pl.ds(HU + j * 128, 128), pl.ds(b * HU + side * 128, 128)] = gu[
                                half * DH + b * 128 : half * DH + (b + 1) * 128,
                                side * HU + j * 128 : side * HU + (j + 1) * 128,
                            ]
            copy_out(acc.at[1 - p, pl.ds(HU, HU)], send_ref.at[pl.ds(HU, HU)])
            keep_ref[...] = acc[p]
            for copy in copies:
                copy.wait()

        keep, send, total, state["r", f], state["du", f] = call(
            body,
            (),
            [first_bit[f], here(state["c"]), here(state["ct"]), here(state["dy"]), w_up, up_b, w_down],
            [smem()] + [in_vmem()] * 6,
            [
                vmem((FC, D), F32),
                hbm((FC, D), F32),
                sds((1, FC), F32),
                hbm((R, FC), BF16),
                hbm((R, FC), BF16),
            ],
            [in_vmem(), anywhere(), in_vmem(), anywhere(), anywhere()],
            [
                pltpu.VMEM((R, FC), BF16),
                pltpu.VMEM((R, FC), BF16),
                pltpu.VMEM((2, FC, D), F32),
                pltpu.SemaphoreType.DMA((4,)),
            ],
            order=order,
            vmem=20,
        )
        up_sums.append(total)

        def finish(mine, got, order):
            def body(p_ref, m_ref, g_ref, *rest):
                gd_ref, gu_ref = rest[-2:]
                own = pl.program_id(0) == p_ref[0]

                def write(ref, side):
                    gd_ref[...] = ref[pl.ds(0, HU), :]
                    for j in range(HU // 128):
                        for b in range(lanes):
                            gu_ref[pl.ds(b * 128, 128), pl.ds(j * 128, 128)] = ref[
                                pl.ds(HU + j * 128, 128), pl.ds(b * HU + side * 128, 128)
                            ]

                for side in range(2):
                    this = pl.program_id(1) == side

                    @pl.when(own & this)
                    def _(side=side):
                        write(m_ref, side)

                    @pl.when(jnp.logical_not(own) & this)
                    def _(side=side):
                        write(g_ref, side)

            ins, specs, aliases = [first_bit[f], mine, got], [smem(), in_vmem(), in_vmem()], {}
            if "gd" in state:
                aliases = {3: 0, 4: 1}
                ins += [in_hbm(state["gd"]), in_hbm(state["gu"])]
                specs += [anywhere()] * 2
            state["gd"], state["gu"] = call(
                body,
                (2, 2),
                ins,
                specs,
                [hbm((FL, D), F32), hbm((D, FL), F32)],
                [
                    pl.BlockSpec((HU, D), lambda t, s: (t * chunks + f, 0)),
                    pl.BlockSpec((DH, HU), lambda t, s: (t, s * chunks + f)),
                ],
                aliases=aliases,
                order=order,
                vmem=10,
            )

        pieces[f] = Piece(links, plan["dims"][f], keep, send, finish)

    def in_order(refs):
        return jnp.concatenate([ref[:, pl.ds(side * HU, HU)] for side in range(2) for ref in refs], axis=1)

    def dc():
        def body(*refs):
            refs[-1][...] = mm(in_order(refs[:-2]), refs[-2][...], 1, 1)

        rowF = pl.BlockSpec((BR, FC), lambda t: (t, 0))
        (state["dc"],) = call(
            body,
            (steps,),
            [in_hbm(state["du", f]) for f in range(chunks)] + [w_up],
            [rowF] * chunks + [in_vmem()],
            [vmem((R, D), F32)],
            [rowD],
            order=order,
            vmem=16,
        )

    def y():
        def body(*refs):
            refs[-1][...] = mm(in_order(refs[:-2]), refs[-2][...])

        rowF = pl.BlockSpec((BR, FC), lambda t: (t, 0))
        (state["y"],) = call(
            body,
            (steps,),
            [in_hbm(state["r", f]) for f in range(chunks)] + [w_down],
            [rowF] * chunks + [in_vmem()],
            [hbm((R, D), F32)],
            [rowD],
            order=order,
            vmem=16,
        )

    def back2():
        def body(h_ref, dy_ref, ctx_ref, wo_ref, g_ref, e0_ref, e1_ref, dh_ref, dctx_ref, go_ref, sum_ref):
            step = pl.program_id(0)
            e = e0_ref[...] + e1_ref[...]
            n, inverse = normed(h_ref[...].astype(F32))
            dh = dy_ref[...].astype(F32) + norm_back(e, n, inverse, g_ref[...])
            dhr = dh.astype(BF16)
            dh_ref[...] = dhr
            dctx_ref[...] = mm(dhr, wo_ref[...], 1, 1).astype(BF16)
            sum_ref[0, 0:1] = colsum(e * n)
            sum_ref[0, 1:2] = colsum(e)
            sum_ref[0, 2:3] = colsum(dhr.astype(F32))
            go = mm(ctx_ref[...], dhr, 0, 0)

            @pl.when(step == 0)
            def _():
                go_ref[...] = go

            @pl.when(step > 0)
            def _():
                go_ref[...] += go

        state["dh"], state["dctx"], state["go"], state["back2"] = call(
            body,
            (steps,),
            [in_hbm(state["h"]), here(state["dy"]), in_hbm(state["ctx"]), w_out, g2]
            + [here(state["dc"]), here(state["dc_got"])],
            [rowD, rowD, rowW, in_vmem(), in_vmem(), rowD, rowD],
            [hbm((R, D), BF16), vmem((R, W), BF16), sds((W, D), F32), sds((steps, 3, D), F32)],
            [rowD, rowW, whole((W, D)), pl.BlockSpec((1, 3, D), lambda t: (t, 0, 0))],
            order=order,
            vmem=20,
        )

    def attn_back():
        def body(pr_ref, qkv_ref, dctx_ref, dqkv_ref, sum_ref):
            lane = lax.broadcasted_iota(jnp.int32, (SP, 128), 1)
            zero = jnp.zeros((SP, 128), BF16)
            for i in range(IB):
                rows = pl.ds(i * SP, SP)
                for j in range(pairs):
                    q = qkv_ref[rows, pl.ds(j * 128, 128)] * jnp.asarray(scale, BF16)
                    k = qkv_ref[rows, pl.ds(W + j * 128, 128)]
                    v = qkv_ref[rows, pl.ds(2 * W + j * 128, 128)]
                    dctx = dctx_ref[rows, pl.ds(j * 128, 128)]
                    dq = dk = dv = None
                    for s in range(2):
                        mine = (lane < 64) if s == 0 else (lane >= 64)
                        pr = pr_ref[i, 2 * j + s]
                        dc = jnp.where(mine, dctx, zero)
                        dv_h = mm(pr, dc)
                        dp = mm(v, dc, 1, 1)
                        p = pr.astype(F32)
                        pdp = p * dp
                        ds = (pdp - p * jnp.sum(pdp, axis=0, keepdims=True)).astype(BF16)
                        dk_h = mm(ds, jnp.where(mine, q, zero))
                        dq_h = mm(ds, jnp.where(mine, k, zero), 0, 0)
                        dq = dq_h if dq is None else dq + dq_h
                        dk = dk_h if dk is None else dk + dk_h
                        dv = dv_h if dv is None else dv + dv_h
                    dqkv_ref[rows, pl.ds(j * 128, 128)] = (dq * scale).astype(BF16)
                    dqkv_ref[rows, pl.ds(W + j * 128, 128)] = dk.astype(BF16)
                    dqkv_ref[rows, pl.ds(2 * W + j * 128, 128)] = dv.astype(BF16)
            sum_ref[0] = colsum(dqkv_ref[...].astype(F32))

        state["dqkv"], state["qkv_sums"] = call(
            body,
            (steps,),
            [in_hbm(state["pr"]), in_hbm(state["qkv"]), here(state["dctx"])],
            [pl.BlockSpec((IB, heads, SP, SP), lambda t: (t, 0, 0, 0)), row3, rowW],
            [vmem((R, 3 * W), BF16), sds((steps, 1, 3 * W), F32)],
            [row3, pl.BlockSpec((1, 1, 3 * W), lambda t: (t, 0, 0))],
            order=order,
            vmem=20,
        )

    def da():
        def body(d_ref, w_ref, o_ref):
            v = None
            for c in range(3):
                term = mm(d_ref[:, pl.ds(c * W, W)], w_ref[c], 1, 1)
                v = term if v is None else v + term
            o_ref[...] = v

        (state["da"],) = call(
            body,
            (steps,),
            [here(state["dqkv"]), wq],
            [row3, in_vmem()],
            [vmem((R, D), F32)],
            [rowD],
            order=order,
            vmem=16,
        )

    DQ, WH = DH // 2, W // 2

    def packed(v):
        return jnp.concatenate([v[:DQ], v[DQ:]], axis=1)

    def gqkv():
        def body(p3_ref, p4_ref, a_ref, dqkv_ref, go_ref, k3_ref, s3_ref, k4_ref, s4_ref, at, tmp):
            step = pl.program_id(0)
            p = p3_ref[0]
            p4 = p4_ref[0]

            @pl.when(step == 0)
            def _():
                at[...] = a_ref[...].T

            @pl.when(step < 3)
            def _():
                g = mm(at[...], dqkv_ref[...])
                tmp[0] = packed(g[:DH])
                tmp[1] = packed(g[DH:])

            @pl.when(step < 2)
            def _():
                k3_ref[...] = tmp[p]
                s3_ref[...] = tmp[1 - p]

            @pl.when(step == 2)
            def _():
                k4_ref[...] = tmp[p4]
                s4_ref[...] = tmp[1 - p4]

            @pl.when(step == 3)
            def _():
                k4_ref[...] = go_ref[pl.ds(pl.multiple_of(p4 * WH, 8), WH), :]
                s4_ref[...] = go_ref[pl.ds(pl.multiple_of((1 - p4) * WH, 8), WH), :]

        first = pl.BlockSpec((DQ, D), lambda t: (jnp.minimum(t, 1), 0))
        second_half = pl.BlockSpec((DQ, D), lambda t: (jnp.maximum(t - 2, 0), 0))
        k3, s3, k4, s4 = call(
            body,
            (4,),
            [first_bit[chunks], first_bit[chunks + 1], state["a"], here(state["dqkv"]), state["go"]],
            [smem(), smem(), in_vmem(), pl.BlockSpec((R, W), lambda t: (0, jnp.minimum(t, 2))), in_vmem()],
            [vmem((DH, D), F32)] * 4,
            [first, first, second_half, second_half],
            [pltpu.VMEM((D, R), BF16), pltpu.VMEM((2, DQ, D), F32)],
            order=order,
            vmem=20,
        )

        def finish3(mine, got, order):
            def body(p_ref, m_ref, g_ref, *rest):
                o_ref = rest[-1]
                own = pl.program_id(0) == p_ref[0]

                def write(ref):
                    for c in range(2):
                        for b in range(2):
                            o_ref[c, pl.ds(b * DQ, DQ), :] = ref[pl.ds(c * DQ, DQ), pl.ds(b * W, W)]

                @pl.when(own)
                def _():
                    write(m_ref)

                @pl.when(jnp.logical_not(own))
                def _():
                    write(g_ref)

            ins, specs, aliases = [first_bit[chunks], mine, got], [smem(), in_vmem(), in_vmem()], {}
            if "gqkv" in state:
                aliases = {3: 0}
                ins += [in_hbm(state["gqkv"])]
                specs += [anywhere()]
            (state["gqkv"],) = call(
                body, (2,), ins, specs, [hbm((3, D, W), F32)],
                [pl.BlockSpec((2, DH, W), lambda t: (0, t, 0))], aliases=aliases, order=order, vmem=10,
            )

        def finish4(mine, got, order):
            def body(p_ref, m_ref, g_ref, *rest):
                o_ref, go_ref = rest[-2:]
                own = pl.program_id(0) == p_ref[0]

                def write(ref):
                    for b in range(2):
                        o_ref[0, pl.ds(b * DQ, DQ), :] = ref[pl.ds(0, DQ), pl.ds(b * W, W)]
                    go_ref[...] = ref[pl.ds(DQ, WH), :]

                @pl.when(own)
                def _():
                    write(m_ref)

                @pl.when(jnp.logical_not(own))
                def _():
                    write(g_ref)

            ins, specs, aliases = [first_bit[chunks + 1], mine, got], [smem(), in_vmem(), in_vmem()], {}
            if "gqkv" in state:
                aliases = {3: 0}
                ins += [in_hbm(state["gqkv"])]
                specs += [anywhere()]
            state["gqkv"], state["grad_out"] = call(
                body, (2,), ins, specs, [hbm((3, D, W), F32), hbm((W, D), F32)],
                [pl.BlockSpec((1, DH, W), lambda t: (2, t, 0)), pl.BlockSpec((WH, D), lambda t: (t, 0))],
                aliases=aliases, order=order, vmem=10,
            )

        def start():
            first, second = release([s3, s4], vmem)
            pieces[chunks] = Piece(links, plan["dims"][chunks], k3, first, finish3)
            pieces[chunks + 1] = Piece(links, plan["dims"][chunks + 1], k4, second, finish4)

        state["qkv_send"] = start

    def gather_rows(ys, o_ref):
        @pl.when(pl.program_id(0) == steps - 1)
        def _():
            for k in range(D // 128):
                v = ys[k, pl.ds(0, seq * items), :].reshape(seq, items, 128)
                o_ref[:, :, pl.ds(k * 128, 128)] = v.astype(BF16)

    def put_rows(ys, v):
        step = pl.program_id(0)
        for j in range(steps):

            @pl.when(step == j)
            def _(j=j):
                for i in range(IB):
                    for k in range(D // 128):
                        ys[k, pl.ds(j * IB + i, SP, stride=items), :] = v[
                            i * SP : (i + 1) * SP, k * 128 : (k + 1) * 128
                        ]

    def back1():
        def body(x_ref, dh_ref, g_ref, e0_ref, e1_ref, o_ref, sum_ref, ys):
            e = e0_ref[...] + e1_ref[...]
            n, inverse = normed(x_ref[...].astype(F32))
            dx = dh_ref[...].astype(F32) + norm_back(e, n, inverse, g_ref[...])
            put_rows(ys, dx)
            sum_ref[0, 0:1] = colsum(e * n)
            sum_ref[0, 1:2] = colsum(e)
            gather_rows(ys, o_ref)

        state["grad_tokens"], state["back1"] = call(
            body,
            (steps,),
            [in_hbm(state["x_kept"]), in_hbm(state["dh"]), g1, here(state["da"]), here(state["da_got"])],
            [rowD, rowD, in_vmem(), rowD, rowD],
            [hbm((seq, items, D), BF16), sds((steps, 2, D), F32)],
            [whole((seq, items, D)), pl.BlockSpec((1, 2, D), lambda t: (t, 0, 0))],
            [pltpu.VMEM((D // 128, SP * items, 128), F32)],
            order=order,
            vmem=24,
        )

    def out():
        def body(cnt_ref, h_ref, p_ref, r_ref, b_ref, o_ref, ys):
            step = pl.program_id(0)
            v = h_ref[...].astype(F32) + (p_ref[...] + r_ref[...]) + b_ref[...]
            item = step * IB + lax.broadcasted_iota(jnp.int32, (BR, D), 0) // SP
            put_rows(ys, jnp.where(item < cnt_ref[0], v, 0.0))
            gather_rows(ys, o_ref)

        (state["output"],) = call(
            body,
            (steps,),
            [item_counts, in_hbm(state["h"]), in_hbm(state["y"]), in_hbm(state["y_got"]), down_b],
            [smem(), rowD, rowD, rowD, in_vmem()],
            [hbm((seq, items, D), BF16)],
            [whole((seq, items, D))],
            [pltpu.VMEM((D // 128, SP * items, 128), F32)],
            order=order,
            vmem=24,
        )

    SR = 16

    def gather():
        def body(q_ref, b2_ref, dy_ref, b1_ref, *rest):
            ups, o_ref = rest[:-1], rest[-1]
            o_ref[...] = jnp.zeros((SR, D), F32)
            qs = jnp.sum(q_ref[...], axis=0)
            o_ref[0:1, pl.ds(0, W)] = qs[:, :W]
            o_ref[0:1, pl.ds(W, W)] = qs[:, 2 * W :]
            o_ref[1:4, :] = jnp.sum(b2_ref[...], axis=0)
            for f in range(chunks):
                for side in range(2):
                    o_ref[4 + side : 5 + side, pl.ds(f * HU, HU)] = ups[f][:, pl.ds(side * HU, HU)]
            o_ref[6:7, :] = dy_ref[...]
            o_ref[7:9, :] = jnp.sum(b1_ref[...], axis=0)

        ins = [state["qkv_sums"], state["back2"], state["dy_sum"], state["back1"]] + up_sums
        state["small"] = call(
            body, (), ins, [in_vmem()] * len(ins), [sds((SR, D), F32)], [in_vmem()], order=order, vmem=8
        )[0]
        state["small_dims"] = [("x", "y"), ("y", "x"), ("a", "a"), ("b", "b")] + [(e, e) for e in links.extra]
        state["small_got"] = links.swap(state["small"], state["small_dims"].pop(0))

    def small():
        if state["small_dims"]:
            state["small"] = add(state["small"], state["small_got"], order)
            state["small_got"] = links.swap(state["small"], state["small_dims"].pop(0))
            return

        def body(a_ref, b_ref, qb_ref, ob_ref, ub_ref, db_ref, gg_ref, gb_ref):
            s = a_ref[...] + b_ref[...]
            qb_ref[0:1, :] = s[0:1, :W]
            qb_ref[1:2, :] = s[0:1, W:]
            gg_ref[1:2, :] = s[1:2]
            gb_ref[1:2, :] = s[2:3]
            ob_ref[...] = s[3:4]
            ub_ref[:, pl.ds(0, D)] = s[4:5]
            ub_ref[:, pl.ds(D, D)] = s[5:6]
            db_ref[...] = s[6:7]
            gg_ref[0:1, :] = s[7:8]
            gb_ref[0:1, :] = s[8:9]

        shapes = [(2, W), (1, D), (1, FL), (1, D), (2, D), (2, D)]
        state["small_outs"] = call(
            body, (), [state["small"], state["small_got"]], [in_vmem()] * 2,
            [sds(v, F32) for v in shapes], [in_vmem()] * len(shapes), order=order, vmem=8,
        )

    jobs = {
        "dc": dc, "y": y, "back2": back2, "attn": attn_back, "gqkv": gqkv, "da": da, "back1": back1, "out": out,
        "gather": gather, "small": small, "dc_send": dc_send, "da_send": da_send, "y_send": y_send,
        "qkv_send": lambda: state["qkv_send"](),
    }
    for job in plan["order"]:
        if job in jobs:
            jobs[job]()
        elif job.startswith("F"):
            ffn(int(job[1:]))
        else:
            pieces[int(job)].step(order)
    for piece in pieces.values():
        while piece.at < len(piece.stages):
            piece.step(order)
    while "small_outs" not in state:
        small()
    qb, ob, ub, db, gg, gb = state["small_outs"]
    return (
        jnp.transpose(state["output"], by_token),
        jnp.transpose(state["grad_tokens"], by_token),
        jnp.transpose(state["gqkv"], (1, 0, 2)),
        qb,
        state["grad_out"],
        ob.reshape(D),
        state["gu"],
        ub.reshape(FL),
        state["gd"],
        db.reshape(D),
        gg,
        gb,
    )


PLAN = {
    "dims": (("yxa", "xya"), ("axy", "ayx"), ("yxa", "xya"), ("xya", "yxa"), ("xya", "yxa")),
    "order": (
        "F0", "F1", "F2", "dc", "0", "dc_send", "back2", "2", "attn", "1", "0", "gqkv", "qkv_send", "0", "da",
        "da_send", "2", "1", "0", "2", "y", "0", "4", "2", "3", "1", "4", "1", "0", "2", "3", "y_send", "back1",
        "4", "out", "2", "4", "1", "3", "4", "gather", "0", "3", "1", "3", "4", "2", "small", "3", "small", "4",
        "small", "small", "1", "3",
    ),
}


def solution(mesh):
    links = Links(mesh.shape["dp"], mesh.shape["tensor"])

    def layer(*arrays):
        return on_device(links, PLAN, *arrays)

    return jax.shard_map(
        layer,
        mesh=mesh,
        in_specs=(
            P("dp", None, None),
            P("dp", None, None),
            P("dp"),
            P("dp"),
            P(None, None, "tensor"),
            P(None, "tensor"),
            P("tensor", None),
            P(),
            P(None, "tensor"),
            P("tensor"),
            P("tensor", None),
            P(),
            P(),
            P(),
        ),
        out_specs=(
            P("dp", None, None),
            P("dp", None, None),
            P(None, None, "tensor"),
            P(None, "tensor"),
            P("tensor", None),
            P(),
            P(None, "tensor"),
            P("tensor"),
            P("tensor", None),
            P(),
            P(),
            P(),
        ),
        check_vma=False,
    )
```

```python
import jax
import jax.numpy as jnp
from jax import lax
from jax.experimental import pallas as pl
from jax.experimental.pallas import tpu as pltpu
from jax.sharding import PartitionSpec as P

HEAD_DIM = 64
PATCHES = 144
EPS = 1e-05
MIB = 1024 * 1024
COST = 1024
F32 = jnp.float32
BF16 = jnp.bfloat16


def mm(a, b, da=1, db=0):
    return lax.dot_general(a, b, (((da,), (db,)), ((), ())), preferred_element_type=F32)


def whole(shape):
    return pl.BlockSpec(shape, lambda *_: (0,) * len(shape))


def anywhere():
    return pl.BlockSpec(memory_space=pl.ANY)


def smem():
    return pl.BlockSpec(memory_space=pltpu.SMEM)


def in_hbm(v):
    return pltpu.with_memory_space_constraint(v, pltpu.HBM)


def here(v):
    return pltpu.with_memory_space_constraint(v, pltpu.VMEM)


class Order:
    def __init__(self):
        self.last = ()


def call(body, grid, ins, in_specs, outs, out_specs, scratch=(), aliases=None, order=None, vmem=24):
    n_in, n_out = len(ins), len(outs)

    def kernel(*refs):
        after_in = n_in + len(order.last)
        body(*refs[:n_in], *refs[after_in : after_in + n_out], *refs[after_in + n_out + 1 :])

    *res, token = pl.pallas_call(
        kernel,
        grid=grid,
        in_specs=list(in_specs) + [anywhere()] * len(order.last),
        out_specs=list(out_specs) + [anywhere()],
        out_shape=list(outs) + [pltpu.HBM((8, 128), F32)],
        scratch_shapes=list(scratch),
        input_output_aliases=aliases or {},
        compiler_params=pltpu.CompilerParams(vmem_limit_bytes=vmem * MIB),
        cost_estimate=pl.CostEstimate(flops=COST, bytes_accessed=COST, transcendentals=0),
    )(*ins, *[in_hbm(v) for v in order.last])
    order.last = (token,)
    return res


def sds(shape, dtype):
    return jax.ShapeDtypeStruct(shape, dtype)


def normed(v):
    centred = v - jnp.mean(v, axis=-1, keepdims=True)
    inverse = lax.rsqrt(jnp.mean(centred * centred, axis=-1, keepdims=True) + EPS)
    return centred * inverse, inverse


def norm_back(e, n, inverse, gain):
    eg = e * gain
    return inverse * (
        eg - jnp.mean(eg, axis=-1, keepdims=True) - n * jnp.mean(eg * n, axis=-1, keepdims=True)
    )


def colsum(v):
    return jnp.sum(v, axis=0, keepdims=True)


def in_vmem():
    return pl.BlockSpec(memory_space=pltpu.VMEM)


BITS = {"x": 0, "y": 1, "a": 2, "b": 3}
HALVING = ("x", "y", "a", "b")


hbm = pltpu.HBM
vmem = pltpu.VMEM


class Links:
    def __init__(self, n_dp, n_t):
        self.n_dp, self.n_t = n_dp, n_t
        self.extra = tuple(range(4, n_dp.bit_length() - 1))

    def swap(self, v, dims):
        pairs = [
            (d * self.n_t + t, (d ^ (1 << BITS.get(dims[t % 2], dims[t % 2]))) * self.n_t + t)
            for d in range(self.n_dp)
            for t in range(self.n_t)
        ]
        return lax.ppermute(v, ("dp", "tensor"), pairs)

    def table(self):
        d, t = lax.axis_index("dp"), lax.axis_index("tensor") % 2
        return [
            ((d >> jnp.where(t == 0, BITS[v], BITS[w])) & 1).reshape(1) for v in HALVING for w in HALVING
        ]

    def place(self, dims):
        return HALVING.index(dims[0]) * 4 + HALVING.index(dims[1])


def add_split(keep, got, side_of, order):
    n, width = keep.shape
    h = n // 2

    def body(b_ref, k_ref, r_ref, ko_ref, so_ref):
        side = b_ref[0]
        mine = pl.ds(pl.multiple_of(side * h, 8), h)
        rest = pl.ds(pl.multiple_of((1 - side) * h, 8), h)
        so_ref[...] = k_ref[rest, :] + r_ref[rest, :]
        ko_ref[...] = k_ref[mine, :] + r_ref[mine, :]

    return call(
        body, (), [side_of, keep, got], [smem(), in_vmem(), in_vmem()],
        [sds((h, width), F32)] * 2, [in_vmem()] * 2, order=order, vmem=5,
    )


def add(keep, got, order):
    def body(k_ref, r_ref, o_ref):
        o_ref[...] = k_ref[...] + r_ref[...]

    return call(
        body, (), [keep, got], [in_vmem()] * 2, [sds(keep.shape, F32)], [in_vmem()], order=order, vmem=5
    )[0]


def join(mine, got, side_of, order):
    n, width = mine.shape

    def body(b_ref, m_ref, r_ref, o_ref):
        side = b_ref[0]
        o_ref[pl.ds(pl.multiple_of(side * n, 8), n), :] = m_ref[...]
        o_ref[pl.ds(pl.multiple_of((1 - side) * n, 8), n), :] = r_ref[...]

    return call(
        body, (), [side_of, mine, got], [smem(), in_vmem(), in_vmem()],
        [sds((2 * n, width), F32)], [in_vmem()], order=order, vmem=5,
    )[0]


class Piece:
    def __init__(self, links, sides, dims, keep, send, finish):
        self.links, self.sides, self.finish = links, sides, finish
        *halving, last = zip(*dims)
        whole = [last] + [(e, e) for e in links.extra]
        self.stages = (
            [(d, "half") for d in halving] + [(d, "whole") for d in whole] + [(d, "back") for d in halving[::-1]]
        )
        self.at = 0
        self.keep = keep
        self.got = links.swap(send, halving[0])

    def step(self, order):
        dim, kind = self.stages[self.at]
        self.at += 1
        if self.at == len(self.stages):
            self.finish(self.keep, self.got, order)
            return
        following, next_kind = self.stages[self.at]
        if kind == "back":
            self.keep = send = join(self.keep, self.got, self.sides[self.links.place(dim)], order)
        elif next_kind == "half":
            self.keep, send = add_split(self.keep, self.got, self.sides[self.links.place(following)], order)
        else:
            self.keep = send = add(self.keep, self.got, order)
        self.got = self.links.swap(send, following)


def on_device(
    links,
    plan,
    tokens,
    cotangent,
    caption_lengths,
    item_counts,
    w_qkv,
    qv_bias,
    w_out,
    out_bias,
    w_up,
    up_bias,
    w_down,
    down_bias,
    ln_gains,
    ln_biases,
):
    order = Order()
    sides = links.table()
    first = [sides[links.place((v[0][0], v[1][0]))] for v in plan["dims"]]
    items, seq, D = tokens.shape
    W = w_qkv.shape[2]
    FL = w_up.shape[1]
    pairs = W // 128
    heads = W // HEAD_DIM
    SP = -(-seq // 64) * 64
    R = items * SP
    IB = 2
    BR = IB * SP
    steps = items // IB
    scale = HEAD_DIM ** (-0.5)

    wq = jnp.transpose(w_qkv, (1, 0, 2))
    bias3 = jnp.concatenate([qv_bias[0], jnp.zeros((W,), F32), qv_bias[1]]).reshape(1, 3 * W)
    g1, g2 = ln_gains[0:1], ln_gains[1:2]
    b1, b2 = ln_biases[0:1], ln_biases[1:2]
    out_b = out_bias.reshape(1, D)
    down_b = down_bias.reshape(1, D)
    up_b = up_bias.reshape(1, FL)
    by_token = (1, 0, 2)
    state = {}
    pieces = {}
    up_sums = []
    swap = [(0, 1), (1, 0)]

    def other(v):
        return lax.ppermute(v, "tensor", swap)

    rowD = pl.BlockSpec((BR, D), lambda t: (t, 0))
    rowW = pl.BlockSpec((BR, W), lambda t: (t, 0))
    row3 = pl.BlockSpec((BR, 3 * W), lambda t: (t, 0))

    def release(arrays, space):
        n = len(arrays)
        return call(
            lambda *refs: None,
            (),
            [pltpu.with_memory_space_constraint(v, space) for v in arrays],
            [anywhere()] * n,
            [space(v.shape, v.dtype) for v in arrays],
            [anywhere()] * n,
            aliases={i: i for i in range(n)},
            order=order,
            vmem=4,
        )

    def dc_send():
        state["dc"] = release([state["dc"]], vmem)[0]
        state["dc_got"] = other(state["dc"])

    def da_send():
        state["da"] = release([state["da"]], vmem)[0]
        state["da_got"] = other(state["da"])

    def y_send():
        state["y"] = release([state["y"]], vmem)[0]
        state["y_got"] = other(state["y"])

    def spread(name, source, masked):
        def body(cnt_ref, *rest):
            t_ref, o_ref, sum_ref, xs = rest[-4:]
            for k in range(D // 128):
                cols = pl.ds(k * 128, 128)
                xs[k, pl.ds(0, seq * items), :] = t_ref[:, :, cols].astype(F32).reshape(seq * items, 128)
                xs[k, pl.ds(seq * items, (SP - seq) * items), :] = jnp.zeros(((SP - seq) * items, 128), F32)
                total = jnp.zeros((1, 128), F32)
                for i in range(items):
                    v = xs[k, pl.ds(i, SP, stride=items), :]
                    if masked:
                        v = jnp.where(i < cnt_ref[0], v, 0.0)
                        total = total + colsum(v)
                    o_ref[pl.ds(i * SP, SP), cols] = v.astype(BF16)
                sum_ref[:, cols] = total

        state[name], state[name + "_sum"] = call(
            body,
            (),
            [item_counts, *sides, jnp.transpose(source, by_token)],
            [smem()] * (1 + len(sides)) + [in_vmem()],
            [vmem((R, D), BF16), sds((1, D), F32)],
            [in_vmem()] * 2,
            [pltpu.VMEM((D // 128, SP * items, 128), F32)],
            order=order,
            vmem=8,
        )

    IH = items // 2
    RH = R // 2

    def attn_fwd(half):
        off = half * RH
        names = ("a", "qkv", "pr", "ctx", "x_kept")

        def body(len_ref, x_ref, wq_ref, b3_ref, g_ref, b_ref, wo_ref, *rest):
            part_ref, a_out, qkv_out, pr_out, ctx_out, x_out, a_ref, qkv_ref, pr_ref, ctx_ref, sems = rest[-11:]
            mine = pl.ds(off, RH)
            copies = []

            def copy_out(source, target):
                copy = pltpu.make_async_copy(source, target, sems.at[len(copies)])
                copy.start()
                copies.append(copy)

            copy_out(x_ref.at[mine], x_out.at[mine])
            n, _ = normed(x_ref[mine, :].astype(F32))
            a = (n * g_ref[...] + b_ref[...]).astype(BF16)
            a_ref[...] = a
            copy_out(a_ref, a_out.at[mine])
            for c in range(3):
                cols = pl.ds(c * W, W)
                qkv_ref[:, cols] = (mm(a, wq_ref[c]) + b3_ref[:, cols]).astype(BF16)
            copy_out(qkv_ref, qkv_out.at[mine])
            lane = lax.broadcasted_iota(jnp.int32, (SP, 128), 1)
            key_at = lax.broadcasted_iota(jnp.int32, (SP, SP), 0)
            zero = jnp.zeros((SP, 128), BF16)
            for i in range(IH):
                valid = key_at < PATCHES + 1 + len_ref[half * IH + i]
                rows = pl.ds(i * SP, SP)
                for j in range(pairs):
                    q = qkv_ref[rows, pl.ds(j * 128, 128)] * jnp.asarray(scale, BF16)
                    k = qkv_ref[rows, pl.ds(W + j * 128, 128)]
                    v = qkv_ref[rows, pl.ds(2 * W + j * 128, 128)]
                    ctx = None
                    for s in range(2):
                        side = (lane < 64) if s == 0 else (lane >= 64)
                        st = mm(k, jnp.where(side, q, zero), 1, 1)
                        st = jnp.where(valid, st, -1e30)
                        e = jnp.exp(st - jnp.max(st, axis=0, keepdims=True))
                        pr = (e * (1.0 / jnp.sum(e, axis=0, keepdims=True))).astype(BF16)
                        pr_ref[i, 2 * j + s] = pr
                        c = mm(pr, jnp.where(side, v, zero), 0, 0)
                        ctx = c if ctx is None else ctx + c
                    ctx_ref[rows, pl.ds(j * 128, 128)] = ctx.astype(BF16)
                copy_out(pr_ref.at[i], pr_out.at[half * IH + i])
            copy_out(ctx_ref, ctx_out.at[mine])
            part_ref[...] = mm(ctx_ref[...], wo_ref[...])
            for copy in copies:
                copy.wait()

        ins = [caption_lengths, here(state["x"]), wq, bias3, g1, b1, w_out]
        specs = [smem()] + [in_vmem()] * 6
        outs = [
            vmem((RH, D), F32),
            hbm((R, D), BF16),
            hbm((R, 3 * W), BF16),
            hbm((items, heads, SP, SP), BF16),
            hbm((R, W), BF16),
            hbm((R, D), BF16),
        ]
        aliases = {}
        if half:
            aliases = {len(ins) + n: 1 + n for n in range(5)}
            ins += [in_hbm(state[v]) for v in names]
            specs += [anywhere()] * 5
        part, *kept = call(
            body,
            (),
            ins,
            specs,
            outs,
            [in_vmem()] + [anywhere()] * 5,
            [
                pltpu.VMEM((RH, D), BF16),
                pltpu.VMEM((RH, 3 * W), BF16),
                pltpu.VMEM((IH, heads, SP, SP), BF16),
                pltpu.VMEM((RH, W), BF16),
                pltpu.SemaphoreType.DMA((4 + IH,)),
            ],
            aliases,
            order=order,
            vmem=16,
        )
        state.update(zip(names, kept))
        return part

    spread("x", tokens, False)
    parts, got = [], []
    for half in range(2):
        part = attn_fwd(half)
        parts.append(part)
        got.append(other(part))

    def second(half):
        def body(x_ref, p_ref, r_ref, ob_ref, g_ref, b_ref, *rest):
            h_ref, c_ref, ct_ref = rest[-3:]
            h = x_ref[...].astype(F32) + (p_ref[...] + r_ref[...]) + ob_ref[...]
            h_ref[...] = h.astype(BF16)
            n, _ = normed(h)
            c = (n * g_ref[...] + b_ref[...]).astype(BF16)
            c_ref[...] = c
            ct_ref[...] = c.T

        off = half * (steps // 2)
        row = lambda t: (t + off, 0)
        ins = [state["x"], parts[half], got[half], out_b, g2, b2]
        specs = [pl.BlockSpec((BR, D), row), rowD, rowD, in_vmem(), in_vmem(), in_vmem()]
        outs = [vmem((R, D), BF16), vmem((R, D), BF16), vmem((D, R), BF16)]
        out_specs = [
            pl.BlockSpec((BR, D), row),
            pl.BlockSpec((BR, D), row),
            pl.BlockSpec((D, BR), lambda t: (0, t + off)),
        ]
        names = ("h", "c", "ct")
        aliases = {}
        if half:
            aliases = {len(ins) + n: n for n in range(3)}
            ins += [here(state["h"]), here(state["c"]), here(state["ct"])]
            specs += [anywhere()] * 3
        kept = call(
            body, (steps // 2,), ins, specs, outs, out_specs, (), aliases, order=order, vmem=11
        )
        state.update(zip(names, kept))

    second(0)
    spread("dy", cotangent, True)
    second(1)

    sizes = [128 * v for v in plan["units"]]
    chunks = len(sizes)
    starts = [sum(sizes[:f]) for f in range(chunks)]
    SB = 256
    DH = D // 2
    HL = FL // 2
    blocks = DH // 128

    def ffn(f):
        HU = sizes[f]
        FC = 2 * HU

        def body(p_ref, c_ref, ct_ref, dy_ref, wu_ref, ub_ref, wd_ref, keep_ref, send_ref, sum_ref, r_ref, du_ref, acc):
            p = p_ref[0]
            units = [pl.ds(starts[f] + side * HL, HU) for side in range(2)]
            wu = jnp.concatenate([wu_ref[:, v] for v in units], axis=1)
            wd = jnp.concatenate([wd_ref[v, :] for v in units], axis=0)
            ub = jnp.concatenate([ub_ref[:, v] for v in units], axis=1)
            total = jnp.zeros((1, FC), F32)
            for s in range(R // SB):
                rows = pl.ds(s * SB, SB)
                u = mm(c_ref[rows, :], wu) + ub
                dr = mm(dy_ref[rows, :], wd, 1, 1)
                below = 0.5 + 0.5 * lax.erf(u * (0.5**0.5))
                density = jnp.exp(-0.5 * u * u) * 0.3989422804014327
                r_ref[rows, :] = (u * below).astype(BF16)
                du = (dr * (below + u * density)).astype(BF16)
                du_ref[rows, :] = du
                total = total + colsum(du.astype(F32))
            sum_ref[...] = total
            gd = mm(r_ref[...], dy_ref[...], 0, 0)
            for half in range(2):
                acc[half, pl.ds(0, HU), :] = gd[half * HU : (half + 1) * HU]
            gu = mm(ct_ref[...], du_ref[...])
            for half in range(2):
                for j in range(HU // 128):
                    for b in range(blocks):
                        for side in range(2):
                            acc[half, pl.ds(HU + j * 128, 128), pl.ds((2 * b + side) * 128, 128)] = gu[
                                half * DH + b * 128 : half * DH + (b + 1) * 128,
                                side * HU + j * 128 : side * HU + (j + 1) * 128,
                            ]
            keep_ref[...] = acc[p]
            send_ref[...] = acc[1 - p]

        keep, send, total, state["r", f], state["du", f] = call(
            body,
            (),
            [first[f], here(state["c"]), here(state["ct"]), here(state["dy"]), w_up, up_b, w_down],
            [smem()] + [in_vmem()] * 6,
            [
                vmem((FC, D), F32),
                vmem((FC, D), F32),
                sds((1, FC), F32),
                vmem((R, FC), BF16),
                vmem((R, FC), BF16),
            ],
            [in_vmem()] * 5,
            [pltpu.VMEM((2, FC, D), F32)],
            order=order,
            vmem=10,
        )
        up_sums.append(total)

        def finish(mine, got, order):
            def body(p_ref, m_ref, g_ref, *rest):
                gd_ref, gu_ref = rest[-2:]
                own = pl.program_id(0) == p_ref[0]

                def write(ref, side):
                    gd_ref[...] = ref[pl.ds(0, HU), :]
                    for j in range(HU // 128):
                        for b in range(blocks):
                            gu_ref[pl.ds(b * 128, 128), pl.ds(j * 128, 128)] = ref[
                                pl.ds(HU + j * 128, 128), pl.ds((2 * b + side) * 128, 128)
                            ]

                for side in range(2):
                    this = pl.program_id(1) == side

                    @pl.when(own & this)
                    def _(side=side):
                        write(m_ref, side)

                    @pl.when(jnp.logical_not(own) & this)
                    def _(side=side):
                        write(g_ref, side)

            ins, specs, aliases = [first[f], mine, got], [smem(), in_vmem(), in_vmem()], {}
            if "gd" in state:
                aliases = {3: 0, 4: 1}
                ins += [in_hbm(state["gd"]), in_hbm(state["gu"])]
                specs += [anywhere()] * 2
            state["gd"], state["gu"] = call(
                body,
                (2, 2),
                ins,
                specs,
                [hbm((FL, D), F32), hbm((D, FL), F32)],
                [
                    pl.BlockSpec((HU, D), lambda t, s: ((t * HL + starts[f]) // HU, 0)),
                    pl.BlockSpec((DH, HU), lambda t, s: (t, (s * HL + starts[f]) // HU)),
                ],
                aliases=aliases,
                order=order,
                vmem=10,
            )

        pieces[f] = Piece(links, sides, plan["dims"][f], keep, send, finish)

    def in_order(refs):
        return jnp.concatenate(
            [ref[:, pl.ds(side * hu, hu)] for side in range(2) for ref, hu in zip(refs, sizes)], axis=1
        )

    def dc():
        def body(*refs):
            refs[-1][...] = mm(in_order(refs[:-2]), refs[-2][...], 1, 1)

        rowF = [pl.BlockSpec((BR, 2 * hu), lambda t: (t, 0)) for hu in sizes]
        (state["dc"],) = call(
            body,
            (steps,),
            [here(state["du", f]) for f in range(chunks)] + [w_up],
            rowF + [in_vmem()],
            [vmem((R, D), F32)],
            [rowD],
            order=order,
            vmem=6,
        )

    def y():
        def body(*refs):
            refs[-1][...] = mm(in_order(refs[:-2]), refs[-2][...])

        rowF = [pl.BlockSpec((BR, 2 * hu), lambda t: (t, 0)) for hu in sizes]
        (state["y"],) = call(
            body,
            (steps,),
            [here(state["r", f]) for f in range(chunks)] + [w_down],
            rowF + [in_vmem()],
            [vmem((R, D), F32)],
            [rowD],
            order=order,
            vmem=8,
        )

    def back2():
        def body(h_ref, dy_ref, ctx_ref, wo_ref, g_ref, e0_ref, e1_ref, dh_ref, dctx_ref, go_ref, sum_ref):
            step = pl.program_id(0)
            e = e0_ref[...] + e1_ref[...]
            n, inverse = normed(h_ref[...].astype(F32))
            dh = dy_ref[...].astype(F32) + norm_back(e, n, inverse, g_ref[...])
            dhr = dh.astype(BF16)
            dh_ref[...] = dhr
            dctx_ref[...] = mm(dhr, wo_ref[...], 1, 1).astype(BF16)
            sum_ref[0, 0:1] = colsum(e * n)
            sum_ref[0, 1:2] = colsum(e)
            sum_ref[0, 2:3] = colsum(dhr.astype(F32))
            go = mm(ctx_ref[...], dhr, 0, 0)

            @pl.when(step == 0)
            def _():
                go_ref[...] = go

            @pl.when(step > 0)
            def _():
                go_ref[...] += go

        state["dh"], state["dctx"], state["go"], state["back2"] = call(
            body,
            (steps,),
            [here(state["h"]), here(state["dy"]), in_hbm(state["ctx"]), w_out, g2]
            + [here(state["dc"]), here(state["dc_got"])],
            [rowD, rowD, rowW, in_vmem(), in_vmem(), rowD, rowD],
            [hbm((R, D), BF16), vmem((R, W), BF16), sds((W, D), F32), sds((steps, 3, D), F32)],
            [rowD, rowW, whole((W, D)), pl.BlockSpec((1, 3, D), lambda t: (t, 0, 0))],
            order=order,
            vmem=10,
        )

    def attn_back():
        def body(pr_ref, qkv_ref, dctx_ref, dqkv_ref, sum_ref):
            lane = lax.broadcasted_iota(jnp.int32, (SP, 128), 1)
            zero = jnp.zeros((SP, 128), BF16)
            for i in range(IB):
                rows = pl.ds(i * SP, SP)
                for j in range(pairs):
                    q = qkv_ref[rows, pl.ds(j * 128, 128)] * jnp.asarray(scale, BF16)
                    k = qkv_ref[rows, pl.ds(W + j * 128, 128)]
                    v = qkv_ref[rows, pl.ds(2 * W + j * 128, 128)]
                    dctx = dctx_ref[rows, pl.ds(j * 128, 128)]
                    dq = dk = dv = None
                    for s in range(2):
                        mine = (lane < 64) if s == 0 else (lane >= 64)
                        pr = pr_ref[i, 2 * j + s]
                        dc = jnp.where(mine, dctx, zero)
                        dv_h = mm(pr, dc)
                        dp = mm(v, dc, 1, 1)
                        p = pr.astype(F32)
                        pdp = p * dp
                        ds = (pdp - p * jnp.sum(pdp, axis=0, keepdims=True)).astype(BF16)
                        dk_h = mm(ds, jnp.where(mine, q, zero))
                        dq_h = mm(ds, jnp.where(mine, k, zero), 0, 0)
                        dq = dq_h if dq is None else dq + dq_h
                        dk = dk_h if dk is None else dk + dk_h
                        dv = dv_h if dv is None else dv + dv_h
                    dqkv_ref[rows, pl.ds(j * 128, 128)] = (dq * scale).astype(BF16)
                    dqkv_ref[rows, pl.ds(W + j * 128, 128)] = dk.astype(BF16)
                    dqkv_ref[rows, pl.ds(2 * W + j * 128, 128)] = dv.astype(BF16)
            sum_ref[0] = colsum(dqkv_ref[...].astype(F32))

        state["dqkv"], state["qkv_sums"] = call(
            body,
            (steps,),
            [in_hbm(state["pr"]), in_hbm(state["qkv"]), here(state["dctx"])],
            [pl.BlockSpec((IB, heads, SP, SP), lambda t: (t, 0, 0, 0)), row3, rowW],
            [vmem((R, 3 * W), BF16), sds((steps, 1, 3 * W), F32)],
            [row3, pl.BlockSpec((1, 1, 3 * W), lambda t: (t, 0, 0))],
            order=order,
            vmem=8,
        )

    def da():
        def body(d_ref, w_ref, o_ref):
            v = None
            for c in range(3):
                term = mm(d_ref[:, pl.ds(c * W, W)], w_ref[c], 1, 1)
                v = term if v is None else v + term
            o_ref[...] = v

        (state["da"],) = call(
            body,
            (steps,),
            [here(state["dqkv"]), wq],
            [row3, in_vmem()],
            [vmem((R, D), F32)],
            [rowD],
            order=order,
            vmem=6,
        )

    DQ, WH = DH // 2, W // 2

    def packed(v):
        return jnp.concatenate([v[:DQ], v[DQ:]], axis=1)

    def gqkv():
        def body(p_ref, p4_ref, a_ref, dqkv_ref, go_ref, k3_ref, s3_ref, k4_ref, s4_ref, at, tmp):
            step = pl.program_id(0)
            p = p_ref[0]
            p4 = p4_ref[0]

            @pl.when(step == 0)
            def _():
                at[...] = a_ref[...].T

            @pl.when(step < 3)
            def _():
                g = mm(at[...], dqkv_ref[...])
                tmp[0] = packed(g[:DH])
                tmp[1] = packed(g[DH:])

            @pl.when(step < 2)
            def _():
                k3_ref[...] = tmp[p]
                s3_ref[...] = tmp[1 - p]

            @pl.when(step == 2)
            def _():
                k4_ref[...] = tmp[p4]
                s4_ref[...] = tmp[1 - p4]

            @pl.when(step == 3)
            def _():
                k4_ref[...] = go_ref[pl.ds(pl.multiple_of(p4 * WH, 8), WH), :]
                s4_ref[...] = go_ref[pl.ds(pl.multiple_of((1 - p4) * WH, 8), WH), :]

        first_half = pl.BlockSpec((DQ, D), lambda t: (jnp.minimum(t, 1), 0))
        second_half = pl.BlockSpec((DQ, D), lambda t: (jnp.maximum(t - 2, 0), 0))
        k3, s3, k4, s4 = call(
            body,
            (4,),
            [first[chunks], first[chunks + 1], state["a"], here(state["dqkv"]), state["go"]],
            [smem(), smem(), in_vmem(), pl.BlockSpec((R, W), lambda t: (0, jnp.minimum(t, 2))), in_vmem()],
            [vmem((DH, D), F32)] * 4,
            [first_half, first_half, second_half, second_half],
            [pltpu.VMEM((D, R), BF16), pltpu.VMEM((2, DQ, D), F32)],
            order=order,
            vmem=10,
        )

        def finish3(mine, got, order):
            def body(p_ref, m_ref, g_ref, *rest):
                o_ref = rest[-1]
                own = pl.program_id(0) == p_ref[0]

                def write(ref):
                    for c in range(2):
                        for b in range(2):
                            o_ref[c, pl.ds(b * DQ, DQ), :] = ref[pl.ds(c * DQ, DQ), pl.ds(b * W, W)]

                @pl.when(own)
                def _():
                    write(m_ref)

                @pl.when(jnp.logical_not(own))
                def _():
                    write(g_ref)

            ins, specs, aliases = [first[chunks], mine, got], [smem(), in_vmem(), in_vmem()], {}
            if "gqkv" in state:
                aliases = {3: 0}
                ins += [in_hbm(state["gqkv"])]
                specs += [anywhere()]
            (state["gqkv"],) = call(
                body, (2,), ins, specs, [hbm((3, D, W), F32)],
                [pl.BlockSpec((2, DH, W), lambda t: (0, t, 0))], aliases=aliases, order=order, vmem=10,
            )

        def finish4(mine, got, order):
            def body(p_ref, m_ref, g_ref, *rest):
                o_ref, go_ref = rest[-2:]
                own = pl.program_id(0) == p_ref[0]

                def write(ref):
                    for b in range(2):
                        o_ref[0, pl.ds(b * DQ, DQ), :] = ref[pl.ds(0, DQ), pl.ds(b * W, W)]
                    go_ref[...] = ref[pl.ds(DQ, WH), :]

                @pl.when(own)
                def _():
                    write(m_ref)

                @pl.when(jnp.logical_not(own))
                def _():
                    write(g_ref)

            ins, specs, aliases = [first[chunks + 1], mine, got], [smem(), in_vmem(), in_vmem()], {}
            if "gqkv" in state:
                aliases = {3: 0}
                ins += [in_hbm(state["gqkv"])]
                specs += [anywhere()]
            state["gqkv"], state["grad_out"] = call(
                body, (2,), ins, specs, [hbm((3, D, W), F32), hbm((W, D), F32)],
                [pl.BlockSpec((1, DH, W), lambda t: (2, t, 0)), pl.BlockSpec((WH, D), lambda t: (t, 0))],
                aliases=aliases, order=order, vmem=10,
            )

        def start():
            send3, send4 = release([s3, s4], vmem)
            pieces[chunks] = Piece(links, sides, plan["dims"][chunks], k3, send3, finish3)
            pieces[chunks + 1] = Piece(links, sides, plan["dims"][chunks + 1], k4, send4, finish4)

        state["qkv_send"] = start

    def gather_rows(ys, o_ref):
        @pl.when(pl.program_id(0) == steps - 1)
        def _():
            for k in range(D // 128):
                v = ys[k, pl.ds(0, seq * items), :].reshape(seq, items, 128)
                o_ref[:, :, pl.ds(k * 128, 128)] = v.astype(BF16)

    def put_rows(ys, v):
        step = pl.program_id(0)
        for j in range(steps):

            @pl.when(step == j)
            def _(j=j):
                for i in range(IB):
                    for k in range(D // 128):
                        ys[k, pl.ds(j * IB + i, SP, stride=items), :] = v[
                            i * SP : (i + 1) * SP, k * 128 : (k + 1) * 128
                        ]

    def back1():
        def body(x_ref, dh_ref, g_ref, e0_ref, e1_ref, o_ref, sum_ref, ys):
            e = e0_ref[...] + e1_ref[...]
            n, inverse = normed(x_ref[...].astype(F32))
            dx = dh_ref[...].astype(F32) + norm_back(e, n, inverse, g_ref[...])
            put_rows(ys, dx)
            sum_ref[0, 0:1] = colsum(e * n)
            sum_ref[0, 1:2] = colsum(e)
            gather_rows(ys, o_ref)

        state["grad_tokens"], state["back1"] = call(
            body,
            (steps,),
            [in_hbm(state["x_kept"]), in_hbm(state["dh"]), g1, here(state["da"]), here(state["da_got"])],
            [rowD, rowD, in_vmem(), rowD, rowD],
            [hbm((seq, items, D), BF16), sds((steps, 2, D), F32)],
            [whole((seq, items, D)), pl.BlockSpec((1, 2, D), lambda t: (t, 0, 0))],
            [pltpu.VMEM((D // 128, SP * items, 128), F32)],
            order=order,
            vmem=17,
        )

    def out():
        def body(cnt_ref, h_ref, p_ref, r_ref, b_ref, o_ref, ys):
            step = pl.program_id(0)
            v = h_ref[...].astype(F32) + (p_ref[...] + r_ref[...]) + b_ref[...]
            item = step * IB + lax.broadcasted_iota(jnp.int32, (BR, D), 0) // SP
            put_rows(ys, jnp.where(item < cnt_ref[0], v, 0.0))
            gather_rows(ys, o_ref)

        (state["output"],) = call(
            body,
            (steps,),
            [item_counts, here(state["h"]), here(state["y"]), here(state["y_got"]), down_b],
            [smem(), rowD, rowD, rowD, in_vmem()],
            [hbm((seq, items, D), BF16)],
            [whole((seq, items, D))],
            [pltpu.VMEM((D // 128, SP * items, 128), F32)],
            order=order,
            vmem=17,
        )

    SR = 16

    def gather():
        def body(q_ref, b2_ref, dy_ref, b1_ref, *rest):
            ups, o_ref = rest[:-1], rest[-1]
            o_ref[...] = jnp.zeros((SR, D), F32)
            qs = jnp.sum(q_ref[...], axis=0)
            o_ref[0:1, pl.ds(0, W)] = qs[:, :W]
            o_ref[0:1, pl.ds(W, W)] = qs[:, 2 * W :]
            o_ref[1:4, :] = jnp.sum(b2_ref[...], axis=0)
            for up, at, hu in zip(ups, starts, sizes):
                for side in range(2):
                    o_ref[4 + side : 5 + side, pl.ds(at, hu)] = up[:, pl.ds(side * hu, hu)]
            o_ref[6:7, :] = dy_ref[...]
            o_ref[7:9, :] = jnp.sum(b1_ref[...], axis=0)

        ins = [state["qkv_sums"], state["back2"], state["dy_sum"], state["back1"]] + up_sums
        state["small"] = call(
            body, (), ins, [in_vmem()] * len(ins), [sds((SR, D), F32)], [in_vmem()], order=order, vmem=8
        )[0]
        state["small_dims"] = [("x", "y"), ("y", "x"), ("a", "a"), ("b", "b")] + [(e, e) for e in links.extra]
        state["small_got"] = links.swap(state["small"], state["small_dims"].pop(0))

    def small():
        if state["small_dims"]:
            state["small"] = add(state["small"], state["small_got"], order)
            state["small_got"] = links.swap(state["small"], state["small_dims"].pop(0))
            return

        def body(a_ref, b_ref, qb_ref, ob_ref, ub_ref, db_ref, gg_ref, gb_ref):
            s = a_ref[...] + b_ref[...]
            qb_ref[0:1, :] = s[0:1, :W]
            qb_ref[1:2, :] = s[0:1, W:]
            gg_ref[1:2, :] = s[1:2]
            gb_ref[1:2, :] = s[2:3]
            ob_ref[...] = s[3]
            ub_ref[pl.ds(0, D)] = s[4]
            ub_ref[pl.ds(D, D)] = s[5]
            db_ref[...] = s[6]
            gg_ref[0:1, :] = s[7:8]
            gb_ref[0:1, :] = s[8:9]

        shapes = [(2, W), (D,), (FL,), (D,), (2, D), (2, D)]
        state["small_outs"] = call(
            body, (), [state["small"], state["small_got"]], [in_vmem()] * 2,
            [sds(v, F32) for v in shapes], [in_vmem()] * len(shapes), order=order, vmem=8,
        )

    jobs = {
        "dc": dc, "y": y, "back2": back2, "attn": attn_back, "gqkv": gqkv, "da": da, "back1": back1, "out": out,
        "gather": gather, "small": small, "dc_send": dc_send, "da_send": da_send, "y_send": y_send,
        "qkv_send": lambda: state["qkv_send"](),
    }
    for job in plan["order"]:
        if job in jobs:
            jobs[job]()
        elif job.startswith("F"):
            ffn(int(job[1:]))
        else:
            pieces[int(job)].step(order)
    for piece in pieces.values():
        while piece.at < len(piece.stages):
            piece.step(order)
    while "small_outs" not in state:
        small()
    qb, ob, ub, db, gg, gb = state["small_outs"]
    return (
        jnp.transpose(state["output"], by_token),
        jnp.transpose(state["grad_tokens"], by_token),
        jnp.transpose(state["gqkv"], (1, 0, 2)),
        qb,
        state["grad_out"],
        ob,
        state["gu"],
        ub,
        state["gd"],
        db,
        gg,
        gb,
    )


PLAN = {
    "units": (1, 1, 2, 2),
    "dims": (("yxab", "xyab"), ("yxab", "xyab"), ("ayxb", "axyb"), ("yxab", "xyab"), ("yxab", "xyab"), ("yxab", "xyab")),
    "order": (
        "F0", "F1", "F2", "F3", "0", "dc", "1", "dc_send", "back2", "attn", "3", "1", "0", "gqkv", "qkv_send", "3",
        "1", "2", "3", "5", "1", "0", "da", "4", "1", "3", "2", "y", "0", "y_send", "4", "5", "2", "3", "da_send",
        "out", "3", "4", "back1", "2", "5", "1", "4", "2", "gather", "0", "5", "4", "1", "0", "small", "5", "3",
        "2", "small", "5", "0", "4", "5", "small", "small", "2", "4",
    ),
}


def solution(mesh):
    links = Links(mesh.shape["dp"], mesh.shape["tensor"])

    def layer(*arrays):
        return on_device(links, PLAN, *arrays)

    return jax.shard_map(
        layer,
        mesh=mesh,
        in_specs=(
            P("dp", None, None),
            P("dp", None, None),
            P("dp"),
            P("dp"),
            P(None, None, "tensor"),
            P(None, "tensor"),
            P("tensor", None),
            P(),
            P(None, "tensor"),
            P("tensor"),
            P("tensor", None),
            P(),
            P(),
            P(),
        ),
        out_specs=(
            P("dp", None, None),
            P("dp", None, None),
            P(None, None, "tensor"),
            P(None, "tensor"),
            P("tensor", None),
            P(),
            P(None, "tensor"),
            P("tensor"),
            P("tensor", None),
            P(),
            P(),
            P(),
        ),
        check_vma=False,
    )
```

```python
import jax
import jax.numpy as jnp
from jax import lax
from jax.experimental import pallas as pl
from jax.experimental.pallas import tpu as pltpu
from jax.sharding import PartitionSpec as P

HEAD_DIM = 64
PATCHES = 144
EPS = 1e-05
MIB = 1024 * 1024
COST = 1024
F32 = jnp.float32
BF16 = jnp.bfloat16


def mm(a, b, da=1, db=0):
    return lax.dot_general(a, b, (((da,), (db,)), ((), ())), preferred_element_type=F32)


def whole(shape):
    return pl.BlockSpec(shape, lambda *_: (0,) * len(shape))


def anywhere():
    return pl.BlockSpec(memory_space=pl.ANY)


def smem():
    return pl.BlockSpec(memory_space=pltpu.SMEM)


def in_hbm(v):
    return pltpu.with_memory_space_constraint(v, pltpu.HBM)


def here(v):
    return pltpu.with_memory_space_constraint(v, pltpu.VMEM)


class Order:
    def __init__(self):
        self.last = ()


def call(body, grid, ins, in_specs, outs, out_specs, scratch=(), aliases=None, order=None, vmem=24):
    n_in, n_out = len(ins), len(outs)

    def kernel(*refs):
        after_in = n_in + len(order.last)
        body(*refs[:n_in], *refs[after_in : after_in + n_out], *refs[after_in + n_out + 1 :])

    *res, token = pl.pallas_call(
        kernel,
        grid=grid,
        in_specs=list(in_specs) + [anywhere()] * len(order.last),
        out_specs=list(out_specs) + [anywhere()],
        out_shape=list(outs) + [pltpu.HBM((8, 128), F32)],
        scratch_shapes=list(scratch),
        input_output_aliases=aliases or {},
        compiler_params=pltpu.CompilerParams(vmem_limit_bytes=vmem * MIB),
        cost_estimate=pl.CostEstimate(flops=COST, bytes_accessed=COST, transcendentals=0),
    )(*ins, *[in_hbm(v) for v in order.last])
    order.last = (token,)
    return res


def sds(shape, dtype):
    return jax.ShapeDtypeStruct(shape, dtype)


def normed(v):
    centred = v - jnp.mean(v, axis=-1, keepdims=True)
    inverse = lax.rsqrt(jnp.mean(centred * centred, axis=-1, keepdims=True) + EPS)
    return centred * inverse, inverse


def norm_back(e, n, inverse, gain):
    eg = e * gain
    return inverse * (
        eg - jnp.mean(eg, axis=-1, keepdims=True) - n * jnp.mean(eg * n, axis=-1, keepdims=True)
    )


def colsum(v):
    return jnp.sum(v, axis=0, keepdims=True)


def in_vmem():
    return pl.BlockSpec(memory_space=pltpu.VMEM)


BITS = {"x": 0, "y": 1, "a": 2, "b": 3}
HALVING = ("x", "y", "a", "b")


hbm = pltpu.HBM
vmem = pltpu.VMEM


class Links:
    def __init__(self, n_dp, n_t):
        self.n_dp, self.n_t = n_dp, n_t
        self.extra = tuple(range(4, n_dp.bit_length() - 1))

    def swap(self, v, dims):
        pairs = [
            (d * self.n_t + t, (d ^ (1 << BITS.get(dims[t % 2], dims[t % 2]))) * self.n_t + t)
            for d in range(self.n_dp)
            for t in range(self.n_t)
        ]
        return lax.ppermute(v, ("dp", "tensor"), pairs)

    def table(self):
        d, t = lax.axis_index("dp"), lax.axis_index("tensor") % 2
        return [
            ((d >> jnp.where(t == 0, BITS[v], BITS[w])) & 1).reshape(1) for v in HALVING for w in HALVING
        ]

    def place(self, dims):
        return HALVING.index(dims[0]) * 4 + HALVING.index(dims[1])


def add_split(keep, got, side_of, order):
    n, width = keep.shape
    h = n // 2

    def body(b_ref, k_ref, r_ref, ko_ref, so_ref):
        side = b_ref[0]
        mine = pl.ds(pl.multiple_of(side * h, 8), h)
        rest = pl.ds(pl.multiple_of((1 - side) * h, 8), h)
        so_ref[...] = k_ref[rest, :] + r_ref[rest, :]
        ko_ref[...] = k_ref[mine, :] + r_ref[mine, :]

    return call(
        body, (), [side_of, keep, got], [smem(), in_vmem(), in_vmem()],
        [sds((h, width), F32)] * 2, [in_vmem()] * 2, order=order, vmem=5,
    )


def add(keep, got, order):
    def body(k_ref, r_ref, o_ref):
        o_ref[...] = k_ref[...] + r_ref[...]

    return call(
        body, (), [keep, got], [in_vmem()] * 2, [sds(keep.shape, F32)], [in_vmem()], order=order, vmem=5
    )[0]


def join(mine, got, side_of, order):
    n, width = mine.shape

    def body(b_ref, m_ref, r_ref, o_ref):
        side = b_ref[0]
        o_ref[pl.ds(pl.multiple_of(side * n, 8), n), :] = m_ref[...]
        o_ref[pl.ds(pl.multiple_of((1 - side) * n, 8), n), :] = r_ref[...]

    return call(
        body, (), [side_of, mine, got], [smem(), in_vmem(), in_vmem()],
        [sds((2 * n, width), F32)], [in_vmem()], order=order, vmem=5,
    )[0]


class Piece:
    def __init__(self, links, sides, dims, keep, send, finish):
        self.links, self.sides, self.finish = links, sides, finish
        *halving, last = zip(*dims)
        whole = [last] + [(e, e) for e in links.extra]
        self.stages = (
            [(d, "half") for d in halving] + [(d, "whole") for d in whole] + [(d, "back") for d in halving[::-1]]
        )
        self.at = 0
        self.keep = keep
        self.got = links.swap(send, halving[0])

    def step(self, order):
        dim, kind = self.stages[self.at]
        self.at += 1
        if self.at == len(self.stages):
            self.finish(self.keep, self.got, order)
            return
        following, next_kind = self.stages[self.at]
        if kind == "back":
            self.keep = send = join(self.keep, self.got, self.sides[self.links.place(dim)], order)
        elif next_kind == "half":
            self.keep, send = add_split(self.keep, self.got, self.sides[self.links.place(following)], order)
        else:
            self.keep = send = add(self.keep, self.got, order)
        self.got = self.links.swap(send, following)


def on_device(
    links,
    plan,
    tokens,
    cotangent,
    caption_lengths,
    item_counts,
    w_qkv,
    qv_bias,
    w_out,
    out_bias,
    w_up,
    up_bias,
    w_down,
    down_bias,
    ln_gains,
    ln_biases,
):
    order = Order()
    sides = links.table()
    first = [sides[links.place((v[0][0], v[1][0]))] for v in plan["dims"]]
    items, seq, D = tokens.shape
    W = w_qkv.shape[2]
    FL = w_up.shape[1]
    pairs = W // 128
    heads = W // HEAD_DIM
    SP = -(-seq // 64) * 64
    R = items * SP
    IB = 2
    BR = IB * SP
    steps = items // IB
    scale = HEAD_DIM ** (-0.5)

    wq = jnp.transpose(w_qkv, (1, 0, 2))
    out_b = out_bias.reshape(1, D)
    down_b = down_bias.reshape(1, D)
    up_b = up_bias.reshape(1, FL)
    by_token = (1, 0, 2)
    state = {}
    pieces = {}
    up_sums = []
    swap = [(0, 1), (1, 0)]

    def other(v):
        return lax.ppermute(v, "tensor", swap)

    rowD = pl.BlockSpec((BR, D), lambda t: (t, 0))
    rowW = pl.BlockSpec((BR, W), lambda t: (t, 0))
    row3 = pl.BlockSpec((BR, 3 * W), lambda t: (t, 0))

    def release(arrays, space):
        n = len(arrays)
        return call(
            lambda *refs: None,
            (),
            [pltpu.with_memory_space_constraint(v, space) for v in arrays],
            [anywhere()] * n,
            [space(v.shape, v.dtype) for v in arrays],
            [anywhere()] * n,
            aliases={i: i for i in range(n)},
            order=order,
            vmem=4,
        )

    def dc_send():
        state["dc"] = release([state["dc"]], vmem)[0]
        state["dc_got"] = other(state["dc"])

    def da_send():
        state["da"] = release([state["da"]], vmem)[0]
        state["da_got"] = other(state["da"])

    def y_send():
        state["y"] = release([state["y"]], vmem)[0]
        state["y_got"] = other(state["y"])

    def spread(name, source, masked):
        def body(cnt_ref, *rest):
            t_ref, o_ref, sum_ref, xs = rest[-4:]
            for k in range(D // 128):
                cols = pl.ds(k * 128, 128)
                xs[k, pl.ds(0, seq * items), :] = t_ref[:, :, cols].astype(F32).reshape(seq * items, 128)
                xs[k, pl.ds(seq * items, (SP - seq) * items), :] = jnp.zeros(((SP - seq) * items, 128), F32)
                total = jnp.zeros((1, 128), F32)
                for i in range(items):
                    v = xs[k, pl.ds(i, SP, stride=items), :]
                    if masked:
                        v = jnp.where(i < cnt_ref[0], v, 0.0)
                        total = total + colsum(v)
                    o_ref[pl.ds(i * SP, SP), cols] = v.astype(BF16)
                sum_ref[:, cols] = total

        state[name], state[name + "_sum"] = call(
            body,
            (),
            [item_counts, *sides, jnp.transpose(source, by_token)],
            [smem()] * (1 + len(sides)) + [in_vmem()],
            [vmem((R, D), BF16), sds((1, D), F32)],
            [in_vmem()] * 2,
            [pltpu.VMEM((D // 128, SP * items, 128), F32)],
            order=order,
            vmem=8,
        )

    IH = items // 2
    RH = R // 2

    def attn_fwd(half):
        off = half * RH
        names = ("a", "qkv", "pr", "ctx", "x_kept")

        def body(len_ref, x_ref, wq_ref, qvb_ref, g_ref, b_ref, wo_ref, *rest):
            part_ref, a_out, qkv_out, pr_out, ctx_out, x_out, a_ref, qkv_ref, pr_ref, ctx_ref, sems = rest[-11:]
            mine = pl.ds(off, RH)
            copies = []

            def copy_out(source, target):
                copy = pltpu.make_async_copy(source, target, sems.at[len(copies)])
                copy.start()
                copies.append(copy)

            copy_out(x_ref.at[mine], x_out.at[mine])
            n, _ = normed(x_ref[mine, :].astype(F32))
            a = (n * g_ref[0:1] + b_ref[0:1]).astype(BF16)
            a_ref[...] = a
            copy_out(a_ref, a_out.at[mine])
            for c in range(3):
                cols = pl.ds(c * W, W)
                v = mm(a, wq_ref[c])
                if c != 1:
                    v = v + qvb_ref[c // 2 : c // 2 + 1]
                qkv_ref[:, cols] = v.astype(BF16)
            copy_out(qkv_ref, qkv_out.at[mine])
            lane = lax.broadcasted_iota(jnp.int32, (SP, 128), 1)
            key_at = lax.broadcasted_iota(jnp.int32, (SP, SP), 0)
            zero = jnp.zeros((SP, 128), BF16)
            for i in range(IH):
                valid = key_at < PATCHES + 1 + len_ref[half * IH + i]
                rows = pl.ds(i * SP, SP)
                for j in range(pairs):
                    q = qkv_ref[rows, pl.ds(j * 128, 128)] * jnp.asarray(scale, BF16)
                    k = qkv_ref[rows, pl.ds(W + j * 128, 128)]
                    v = qkv_ref[rows, pl.ds(2 * W + j * 128, 128)]
                    ctx = None
                    for s in range(2):
                        side = (lane < 64) if s == 0 else (lane >= 64)
                        st = mm(k, jnp.where(side, q, zero), 1, 1)
                        st = jnp.where(valid, st, -1e30)
                        e = jnp.exp(st - jnp.max(st, axis=0, keepdims=True))
                        pr = (e * (1.0 / jnp.sum(e, axis=0, keepdims=True))).astype(BF16)
                        pr_ref[i, 2 * j + s] = pr
                        c = mm(pr, jnp.where(side, v, zero), 0, 0)
                        ctx = c if ctx is None else ctx + c
                    ctx_ref[rows, pl.ds(j * 128, 128)] = ctx.astype(BF16)
                copy_out(pr_ref.at[i], pr_out.at[half * IH + i])
            copy_out(ctx_ref, ctx_out.at[mine])
            part_ref[...] = mm(ctx_ref[...], wo_ref[...])
            for copy in copies:
                copy.wait()

        ins = [in_hbm(caption_lengths), here(state["x"]), wq, in_hbm(qv_bias), in_hbm(ln_gains), in_hbm(ln_biases), w_out]
        specs = [smem()] + [in_vmem()] * 6
        outs = [
            vmem((RH, D), F32),
            hbm((R, D), BF16),
            hbm((R, 3 * W), BF16),
            hbm((items, heads, SP, SP), BF16),
            hbm((R, W), BF16),
            hbm((R, D), BF16),
        ]
        aliases = {}
        if half:
            aliases = {len(ins) + n: 1 + n for n in range(5)}
            ins += [in_hbm(state[v]) for v in names]
            specs += [anywhere()] * 5
        part, *kept = call(
            body,
            (),
            ins,
            specs,
            outs,
            [in_vmem()] + [anywhere()] * 5,
            [
                pltpu.VMEM((RH, D), BF16),
                pltpu.VMEM((RH, 3 * W), BF16),
                pltpu.VMEM((IH, heads, SP, SP), BF16),
                pltpu.VMEM((RH, W), BF16),
                pltpu.SemaphoreType.DMA((4 + IH,)),
            ],
            aliases,
            order=order,
            vmem=16,
        )
        state.update(zip(names, kept))
        return part

    spread("x", tokens, False)
    parts, got = [], []
    for half in range(2):
        part = attn_fwd(half)
        parts.append(part)
        got.append(other(part))

    def second(half):
        def body(x_ref, p_ref, r_ref, ob_ref, g_ref, b_ref, *rest):
            h_ref, c_ref, ct_ref = rest[-3:]
            h = x_ref[...].astype(F32) + (p_ref[...] + r_ref[...]) + ob_ref[...]
            h_ref[...] = h.astype(BF16)
            n, _ = normed(h)
            c = (n * g_ref[1:2] + b_ref[1:2]).astype(BF16)
            c_ref[...] = c
            ct_ref[...] = c.T

        off = half * (steps // 2)
        row = lambda t: (t + off, 0)
        ins = [state["x"], parts[half], got[half], out_b, in_hbm(ln_gains), in_hbm(ln_biases)]
        specs = [pl.BlockSpec((BR, D), row), rowD, rowD, in_vmem(), in_vmem(), in_vmem()]
        outs = [vmem((R, D), BF16), vmem((R, D), BF16), vmem((D, R), BF16)]
        out_specs = [
            pl.BlockSpec((BR, D), row),
            pl.BlockSpec((BR, D), row),
            pl.BlockSpec((D, BR), lambda t: (0, t + off)),
        ]
        names = ("h", "c", "ct")
        aliases = {}
        if half:
            aliases = {len(ins) + n: n for n in range(3)}
            ins += [here(state["h"]), here(state["c"]), here(state["ct"])]
            specs += [anywhere()] * 3
        kept = call(
            body, (steps // 2,), ins, specs, outs, out_specs, (), aliases, order=order, vmem=11
        )
        state.update(zip(names, kept))

    second(0)
    spread("dy", cotangent, True)
    second(1)

    sizes = [128 * v for v in plan["units"]]
    chunks = len(sizes)
    starts = [sum(sizes[:f]) for f in range(chunks)]
    SB = 256
    DH = D // 2
    HL = FL // 2
    blocks = DH // 128

    def ffn(f):
        HU = sizes[f]
        FC = 2 * HU

        def body(p_ref, c_ref, ct_ref, dy_ref, wu_ref, ub_ref, wd_ref, keep_ref, send_ref, sum_ref, r_ref, du_ref, acc):
            p = p_ref[0]
            units = [pl.ds(starts[f] + side * HL, HU) for side in range(2)]
            wu = jnp.concatenate([wu_ref[:, v] for v in units], axis=1)
            wd = jnp.concatenate([wd_ref[v, :] for v in units], axis=0)
            ub = jnp.concatenate([ub_ref[:, v] for v in units], axis=1)
            total = jnp.zeros((1, FC), F32)
            for s in range(R // SB):
                rows = pl.ds(s * SB, SB)
                u = mm(c_ref[rows, :], wu) + ub
                dr = mm(dy_ref[rows, :], wd, 1, 1)
                below = 0.5 + 0.5 * lax.erf(u * (0.5**0.5))
                density = jnp.exp(-0.5 * u * u) * 0.3989422804014327
                r_ref[rows, :] = (u * below).astype(BF16)
                du = (dr * (below + u * density)).astype(BF16)
                du_ref[rows, :] = du
                total = total + colsum(du.astype(F32))
            sum_ref[...] = total
            gd = mm(r_ref[...], dy_ref[...], 0, 0)
            for half in range(2):
                acc[half, pl.ds(0, HU), :] = gd[half * HU : (half + 1) * HU]
            gu = mm(ct_ref[...], du_ref[...])
            for half in range(2):
                for j in range(HU // 128):
                    for b in range(blocks):
                        for side in range(2):
                            acc[half, pl.ds(HU + j * 128, 128), pl.ds((2 * b + side) * 128, 128)] = gu[
                                half * DH + b * 128 : half * DH + (b + 1) * 128,
                                side * HU + j * 128 : side * HU + (j + 1) * 128,
                            ]
            keep_ref[...] = acc[p]
            send_ref[...] = acc[1 - p]

        keep, send, total, state["r", f], state["du", f] = call(
            body,
            (),
            [first[f], here(state["c"]), here(state["ct"]), here(state["dy"]), w_up, up_b, w_down],
            [smem()] + [in_vmem()] * 6,
            [
                vmem((FC, D), F32),
                vmem((FC, D), F32),
                sds((1, FC), F32),
                vmem((R, FC), BF16),
                vmem((R, FC), BF16),
            ],
            [in_vmem()] * 5,
            [pltpu.VMEM((2, FC, D), F32)],
            order=order,
            vmem=10,
        )
        up_sums.append(total)

        def finish(mine, got, order):
            def body(p_ref, m_ref, g_ref, *rest):
                gd_ref, gu_ref = rest[-2:]
                own = pl.program_id(0) == p_ref[0]

                def write(ref, side):
                    gd_ref[...] = ref[pl.ds(0, HU), :]
                    for j in range(HU // 128):
                        for b in range(blocks):
                            gu_ref[pl.ds(b * 128, 128), pl.ds(j * 128, 128)] = ref[
                                pl.ds(HU + j * 128, 128), pl.ds((2 * b + side) * 128, 128)
                            ]

                for side in range(2):
                    this = pl.program_id(1) == side

                    @pl.when(own & this)
                    def _(side=side):
                        write(m_ref, side)

                    @pl.when(jnp.logical_not(own) & this)
                    def _(side=side):
                        write(g_ref, side)

            ins, specs, aliases = [first[f], mine, got], [smem(), in_vmem(), in_vmem()], {}
            if "gd" in state:
                aliases = {3: 0, 4: 1}
                ins += [in_hbm(state["gd"]), in_hbm(state["gu"])]
                specs += [anywhere()] * 2
            state["gd"], state["gu"] = call(
                body,
                (2, 2),
                ins,
                specs,
                [hbm((FL, D), F32), hbm((D, FL), F32)],
                [
                    pl.BlockSpec((HU, D), lambda t, s: ((t * HL + starts[f]) // HU, 0)),
                    pl.BlockSpec((DH, HU), lambda t, s: (t, (s * HL + starts[f]) // HU)),
                ],
                aliases=aliases,
                order=order,
                vmem=10,
            )

        pieces[f] = Piece(links, sides, plan["dims"][f], keep, send, finish)

    def in_order(refs):
        return jnp.concatenate(
            [ref[:, pl.ds(side * hu, hu)] for side in range(2) for ref, hu in zip(refs, sizes)], axis=1
        )

    def dc():
        def body(*refs):
            refs[-1][...] = mm(in_order(refs[:-2]), refs[-2][...], 1, 1)

        rowF = [pl.BlockSpec((BR, 2 * hu), lambda t: (t, 0)) for hu in sizes]
        (state["dc"],) = call(
            body,
            (steps,),
            [here(state["du", f]) for f in range(chunks)] + [w_up],
            rowF + [in_vmem()],
            [vmem((R, D), F32)],
            [rowD],
            order=order,
            vmem=6,
        )

    def y():
        def body(*refs):
            refs[-1][...] = mm(in_order(refs[:-2]), refs[-2][...])

        rowF = [pl.BlockSpec((BR, 2 * hu), lambda t: (t, 0)) for hu in sizes]
        (state["y"],) = call(
            body,
            (steps,),
            [here(state["r", f]) for f in range(chunks)] + [w_down],
            rowF + [in_vmem()],
            [vmem((R, D), F32)],
            [rowD],
            order=order,
            vmem=8,
        )

    def back2():
        def body(h_ref, dy_ref, ctx_ref, wo_ref, g_ref, e0_ref, e1_ref, dh_ref, dctx_ref, go_ref, sum_ref):
            step = pl.program_id(0)
            e = e0_ref[...] + e1_ref[...]
            n, inverse = normed(h_ref[...].astype(F32))
            dh = dy_ref[...].astype(F32) + norm_back(e, n, inverse, g_ref[1:2])
            dhr = dh.astype(BF16)
            dh_ref[...] = dhr
            dctx_ref[...] = mm(dhr, wo_ref[...], 1, 1).astype(BF16)
            sum_ref[0, 0:1] = colsum(e * n)
            sum_ref[0, 1:2] = colsum(e)
            sum_ref[0, 2:3] = colsum(dhr.astype(F32))
            go = mm(ctx_ref[...], dhr, 0, 0)

            @pl.when(step == 0)
            def _():
                go_ref[...] = go

            @pl.when(step > 0)
            def _():
                go_ref[...] += go

        state["dh"], state["dctx"], state["go"], state["back2"] = call(
            body,
            (steps,),
            [here(state["h"]), here(state["dy"]), in_hbm(state["ctx"]), w_out, in_hbm(ln_gains)]
            + [here(state["dc"]), here(state["dc_got"])],
            [rowD, rowD, rowW, in_vmem(), in_vmem(), rowD, rowD],
            [hbm((R, D), BF16), vmem((R, W), BF16), sds((W, D), F32), sds((steps, 3, D), F32)],
            [rowD, rowW, whole((W, D)), pl.BlockSpec((1, 3, D), lambda t: (t, 0, 0))],
            order=order,
            vmem=10,
        )

    def attn_back(half):
        def body(pr_ref, qkv_ref, dctx_ref, *rest):
            dqkv_ref, sum_ref = rest[-2:]
            lane = lax.broadcasted_iota(jnp.int32, (SP, 128), 1)
            zero = jnp.zeros((SP, 128), BF16)
            for i in range(IB):
                rows = pl.ds(i * SP, SP)
                for j in range(pairs):
                    q = qkv_ref[rows, pl.ds(j * 128, 128)] * jnp.asarray(scale, BF16)
                    k = qkv_ref[rows, pl.ds(W + j * 128, 128)]
                    v = qkv_ref[rows, pl.ds(2 * W + j * 128, 128)]
                    dctx = dctx_ref[rows, pl.ds(j * 128, 128)]
                    dq = dk = dv = None
                    for s in range(2):
                        mine = (lane < 64) if s == 0 else (lane >= 64)
                        pr = pr_ref[i, 2 * j + s]
                        dc = jnp.where(mine, dctx, zero)
                        dv_h = mm(pr, dc)
                        dp = mm(v, dc, 1, 1)
                        p = pr.astype(F32)
                        pdp = p * dp
                        ds = (pdp - p * jnp.sum(pdp, axis=0, keepdims=True)).astype(BF16)
                        dk_h = mm(ds, jnp.where(mine, q, zero))
                        dq_h = mm(ds, jnp.where(mine, k, zero), 0, 0)
                        dq = dq_h if dq is None else dq + dq_h
                        dk = dk_h if dk is None else dk + dk_h
                        dv = dv_h if dv is None else dv + dv_h
                    dqkv_ref[rows, pl.ds(j * 128, 128)] = (dq * scale).astype(BF16)
                    dqkv_ref[rows, pl.ds(W + j * 128, 128)] = dk.astype(BF16)
                    dqkv_ref[rows, pl.ds(2 * W + j * 128, 128)] = dv.astype(BF16)
            sum_ref[0] = colsum(dqkv_ref[...].astype(F32))

        off = half * (steps // 2)
        ins = [in_hbm(state["pr"]), in_hbm(state["qkv"]), here(state["dctx"])]
        specs = [
            pl.BlockSpec((IB, heads, SP, SP), lambda t: (t + off, 0, 0, 0)),
            pl.BlockSpec((BR, 3 * W), lambda t: (t + off, 0)),
            pl.BlockSpec((BR, W), lambda t: (t + off, 0)),
        ]
        aliases = {}
        if half:
            aliases = {3: 0, 4: 1}
            ins += [here(state["dqkv"]), here(state["qkv_sums"])]
            specs += [anywhere()] * 2
        state["dqkv"], state["qkv_sums"] = call(
            body,
            (steps // 2,),
            ins,
            specs,
            [vmem((R, 3 * W), BF16), vmem((steps, 1, 3 * W), F32)],
            [
                pl.BlockSpec((BR, 3 * W), lambda t: (t + off, 0)),
                pl.BlockSpec((1, 1, 3 * W), lambda t: (t + off, 0, 0)),
            ],
            aliases=aliases,
            order=order,
            vmem=8,
        )

    def da():
        def body(d_ref, w_ref, o_ref):
            v = None
            for c in range(3):
                term = mm(d_ref[:, pl.ds(c * W, W)], w_ref[c], 1, 1)
                v = term if v is None else v + term
            o_ref[...] = v

        (state["da"],) = call(
            body,
            (steps,),
            [here(state["dqkv"]), wq],
            [row3, in_vmem()],
            [vmem((R, D), F32)],
            [rowD],
            order=order,
            vmem=6,
        )

    DQ, WH = DH // 2, W // 2

    def packed(v):
        return jnp.concatenate([v[:DQ], v[DQ:]], axis=1)

    def gqkv():
        def body(p_ref, p4_ref, a_ref, dqkv_ref, go_ref, k3_ref, s3_ref, k4_ref, s4_ref, at, tmp):
            step = pl.program_id(0)
            p = p_ref[0]
            p4 = p4_ref[0]

            @pl.when(step == 0)
            def _():
                at[...] = a_ref[...].T

            @pl.when(step < 3)
            def _():
                g = mm(at[...], dqkv_ref[...])
                tmp[0] = packed(g[:DH])
                tmp[1] = packed(g[DH:])

            @pl.when(step < 2)
            def _():
                k3_ref[...] = tmp[p]
                s3_ref[...] = tmp[1 - p]

            @pl.when(step == 2)
            def _():
                k4_ref[...] = tmp[p4]
                s4_ref[...] = tmp[1 - p4]

            @pl.when(step == 3)
            def _():
                k4_ref[...] = go_ref[pl.ds(pl.multiple_of(p4 * WH, 8), WH), :]
                s4_ref[...] = go_ref[pl.ds(pl.multiple_of((1 - p4) * WH, 8), WH), :]

        first_half = pl.BlockSpec((DQ, D), lambda t: (jnp.minimum(t, 1), 0))
        second_half = pl.BlockSpec((DQ, D), lambda t: (jnp.maximum(t - 2, 0), 0))
        k3, s3, k4, s4 = call(
            body,
            (4,),
            [first[chunks], first[chunks + 1], state["a"], here(state["dqkv"]), state["go"]],
            [smem(), smem(), in_vmem(), pl.BlockSpec((R, W), lambda t: (0, jnp.minimum(t, 2))), in_vmem()],
            [vmem((DH, D), F32)] * 4,
            [first_half, first_half, second_half, second_half],
            [pltpu.VMEM((D, R), BF16), pltpu.VMEM((2, DQ, D), F32)],
            order=order,
            vmem=10,
        )

        def finish3(mine, got, order):
            def body(p_ref, m_ref, g_ref, *rest):
                o_ref = rest[-1]
                own = pl.program_id(0) == p_ref[0]

                def write(ref):
                    for c in range(2):
                        for b in range(2):
                            o_ref[c, pl.ds(b * DQ, DQ), :] = ref[pl.ds(c * DQ, DQ), pl.ds(b * W, W)]

                @pl.when(own)
                def _():
                    write(m_ref)

                @pl.when(jnp.logical_not(own))
                def _():
                    write(g_ref)

            ins, specs, aliases = [first[chunks], mine, got], [smem(), in_vmem(), in_vmem()], {}
            if "gqkv" in state:
                aliases = {3: 0}
                ins += [in_hbm(state["gqkv"])]
                specs += [anywhere()]
            (state["gqkv"],) = call(
                body, (2,), ins, specs, [hbm((3, D, W), F32)],
                [pl.BlockSpec((2, DH, W), lambda t: (0, t, 0))], aliases=aliases, order=order, vmem=10,
            )

        def finish4(mine, got, order):
            def body(p_ref, m_ref, g_ref, *rest):
                o_ref, go_ref = rest[-2:]
                own = pl.program_id(0) == p_ref[0]

                def write(ref):
                    for b in range(2):
                        o_ref[0, pl.ds(b * DQ, DQ), :] = ref[pl.ds(0, DQ), pl.ds(b * W, W)]
                    go_ref[...] = ref[pl.ds(DQ, WH), :]

                @pl.when(own)
                def _():
                    write(m_ref)

                @pl.when(jnp.logical_not(own))
                def _():
                    write(g_ref)

            ins, specs, aliases = [first[chunks + 1], mine, got], [smem(), in_vmem(), in_vmem()], {}
            if "gqkv" in state:
                aliases = {3: 0}
                ins += [in_hbm(state["gqkv"])]
                specs += [anywhere()]
            state["gqkv"], state["grad_out"] = call(
                body, (2,), ins, specs, [hbm((3, D, W), F32), hbm((W, D), F32)],
                [pl.BlockSpec((1, DH, W), lambda t: (2, t, 0)), pl.BlockSpec((WH, D), lambda t: (t, 0))],
                aliases=aliases, order=order, vmem=10,
            )

        def start():
            send3, send4 = release([s3, s4], vmem)
            pieces[chunks] = Piece(links, sides, plan["dims"][chunks], k3, send3, finish3)
            pieces[chunks + 1] = Piece(links, sides, plan["dims"][chunks + 1], k4, send4, finish4)

        state["qkv_send"] = start

    def gather_rows(ys, o_ref):
        @pl.when(pl.program_id(0) == steps - 1)
        def _():
            for k in range(D // 128):
                v = ys[k, pl.ds(0, seq * items), :].reshape(seq, items, 128)
                o_ref[:, :, pl.ds(k * 128, 128)] = v.astype(BF16)

    def put_rows(ys, v):
        step = pl.program_id(0)
        for j in range(steps):

            @pl.when(step == j)
            def _(j=j):
                for i in range(IB):
                    for k in range(D // 128):
                        ys[k, pl.ds(j * IB + i, SP, stride=items), :] = v[
                            i * SP : (i + 1) * SP, k * 128 : (k + 1) * 128
                        ]

    def back1():
        def body(x_ref, dh_ref, g_ref, e0_ref, e1_ref, o_ref, sum_ref, ys):
            e = e0_ref[...] + e1_ref[...]
            n, inverse = normed(x_ref[...].astype(F32))
            dx = dh_ref[...].astype(F32) + norm_back(e, n, inverse, g_ref[0:1])
            put_rows(ys, dx)
            sum_ref[0, 0:1] = colsum(e * n)
            sum_ref[0, 1:2] = colsum(e)
            gather_rows(ys, o_ref)

        state["grad_tokens"], state["back1"] = call(
            body,
            (steps,),
            [in_hbm(state["x_kept"]), in_hbm(state["dh"]), in_hbm(ln_gains), here(state["da"]), here(state["da_got"])],
            [rowD, rowD, in_vmem(), rowD, rowD],
            [hbm((seq, items, D), BF16), sds((steps, 2, D), F32)],
            [whole((seq, items, D)), pl.BlockSpec((1, 2, D), lambda t: (t, 0, 0))],
            [pltpu.VMEM((D // 128, SP * items, 128), F32)],
            order=order,
            vmem=17,
        )

    def out():
        def body(cnt_ref, h_ref, p_ref, r_ref, b_ref, o_ref, ys):
            step = pl.program_id(0)
            v = h_ref[...].astype(F32) + (p_ref[...] + r_ref[...]) + b_ref[...]
            item = step * IB + lax.broadcasted_iota(jnp.int32, (BR, D), 0) // SP
            put_rows(ys, jnp.where(item < cnt_ref[0], v, 0.0))
            gather_rows(ys, o_ref)

        (state["output"],) = call(
            body,
            (steps,),
            [item_counts, here(state["h"]), here(state["y"]), here(state["y_got"]), down_b],
            [smem(), rowD, rowD, rowD, in_vmem()],
            [hbm((seq, items, D), BF16)],
            [whole((seq, items, D))],
            [pltpu.VMEM((D // 128, SP * items, 128), F32)],
            order=order,
            vmem=17,
        )

    SR = 16

    def gather():
        def body(q_ref, b2_ref, dy_ref, b1_ref, *rest):
            ups, o_ref = rest[:-1], rest[-1]
            o_ref[...] = jnp.zeros((SR, D), F32)
            qs = jnp.sum(q_ref[...], axis=0)
            o_ref[0:1, pl.ds(0, W)] = qs[:, :W]
            o_ref[0:1, pl.ds(W, W)] = qs[:, 2 * W :]
            o_ref[1:4, :] = jnp.sum(b2_ref[...], axis=0)
            for up, at, hu in zip(ups, starts, sizes):
                for side in range(2):
                    o_ref[4 + side : 5 + side, pl.ds(at, hu)] = up[:, pl.ds(side * hu, hu)]
            o_ref[6:7, :] = dy_ref[...]
            o_ref[7:9, :] = jnp.sum(b1_ref[...], axis=0)

        ins = [state["qkv_sums"], state["back2"], state["dy_sum"], state["back1"]] + up_sums
        state["small"] = call(
            body, (), ins, [in_vmem()] * len(ins), [sds((SR, D), F32)], [in_vmem()], order=order, vmem=8
        )[0]
        state["small_dims"] = [("x", "y"), ("y", "x"), ("a", "a"), ("b", "b")] + [(e, e) for e in links.extra]
        state["small_got"] = links.swap(state["small"], state["small_dims"].pop(0))

    def small():
        if state["small_dims"]:
            state["small"] = add(state["small"], state["small_got"], order)
            state["small_got"] = links.swap(state["small"], state["small_dims"].pop(0))
            return

        def body(a_ref, b_ref, qb_ref, ob_ref, ub_ref, db_ref, gg_ref, gb_ref):
            s = a_ref[...] + b_ref[...]
            qb_ref[0:1, :] = s[0:1, :W]
            qb_ref[1:2, :] = s[0:1, W:]
            gg_ref[1:2, :] = s[1:2]
            gb_ref[1:2, :] = s[2:3]
            ob_ref[...] = s[3]
            ub_ref[pl.ds(0, D)] = s[4]
            ub_ref[pl.ds(D, D)] = s[5]
            db_ref[...] = s[6]
            gg_ref[0:1, :] = s[7:8]
            gb_ref[0:1, :] = s[8:9]

        shapes = [(2, W), (D,), (FL,), (D,), (2, D), (2, D)]
        state["small_outs"] = call(
            body, (), [state["small"], state["small_got"]], [in_vmem()] * 2,
            [sds(v, F32) for v in shapes], [in_vmem()] * len(shapes), order=order, vmem=8,
        )

    jobs = {
        "dc": dc, "y": y, "back2": back2, "attn": lambda: attn_back(0), "attn2": lambda: attn_back(1), "gqkv": gqkv, "da": da, "back1": back1, "out": out,
        "gather": gather, "small": small, "dc_send": dc_send, "da_send": da_send, "y_send": y_send,
        "qkv_send": lambda: state["qkv_send"](),
    }
    for job in plan["order"]:
        if job in jobs:
            jobs[job]()
        elif job.startswith("F"):
            ffn(int(job[1:]))
        else:
            pieces[int(job)].step(order)
    for piece in pieces.values():
        while piece.at < len(piece.stages):
            piece.step(order)
    while "small_outs" not in state:
        small()
    qb, ob, ub, db, gg, gb = state["small_outs"]
    return (
        jnp.transpose(state["output"], by_token),
        jnp.transpose(state["grad_tokens"], by_token),
        jnp.transpose(state["gqkv"], (1, 0, 2)),
        qb,
        state["grad_out"],
        ob,
        state["gu"],
        ub,
        state["gd"],
        db,
        gg,
        gb,
    )


PLAN = {
    "units": (1, 1, 2, 2),
    "dims": (("xyab", "yxab"), ("xyba", "yxba"), ("yxab", "xyab"), ("ayxb", "axyb"), ("yxab", "xyab"), ("yxab", "xyab")),
    "order": (
        "F0", "F1", "F2", "F3", "dc", "0", "1", "dc_send", "back2", "attn", "2", "attn2", "gqkv", "0", "1",
        "qkv_send", "2", "3", "da", "2", "da_send", "1", "5", "3", "y", "0", "2", "1", "0", "5", "4", "2", "3",
        "y_send", "back1", "5", "2", "4", "out", "3", "0", "4", "gather", "5", "3", "0", "4", "small", "5", "5",
        "3", "4", "2", "small", "1", "1", "0", "4", "5", "3", "small", "1", "small", "4",
    ),
}


def solution(mesh):
    links = Links(mesh.shape["dp"], mesh.shape["tensor"])

    def layer(*arrays):
        return on_device(links, PLAN, *arrays)

    return jax.shard_map(
        layer,
        mesh=mesh,
        in_specs=(
            P("dp", None, None),
            P("dp", None, None),
            P("dp"),
            P("dp"),
            P(None, None, "tensor"),
            P(None, "tensor"),
            P("tensor", None),
            P(),
            P(None, "tensor"),
            P("tensor"),
            P("tensor", None),
            P(),
            P(),
            P(),
        ),
        out_specs=(
            P("dp", None, None),
            P("dp", None, None),
            P(None, None, "tensor"),
            P(None, "tensor"),
            P("tensor", None),
            P(),
            P(None, "tensor"),
            P("tensor"),
            P("tensor", None),
            P(),
            P(),
            P(),
        ),
        check_vma=False,
    )
```

```python
import jax
import jax.numpy as jnp
from jax import lax
from jax.experimental import pallas as pl
from jax.experimental.pallas import tpu as pltpu
from jax.sharding import PartitionSpec as P

HEAD_DIM = 64
PATCHES = 144
EPS = 1e-05
MIB = 1024 * 1024
COST = 1024
F32 = jnp.float32
BF16 = jnp.bfloat16


def mm(a, b, da=1, db=0):
    return lax.dot_general(a, b, (((da,), (db,)), ((), ())), preferred_element_type=F32)


def whole(shape):
    return pl.BlockSpec(shape, lambda *_: (0,) * len(shape))


def anywhere():
    return pl.BlockSpec(memory_space=pl.ANY)


def smem():
    return pl.BlockSpec(memory_space=pltpu.SMEM)


def in_hbm(v):
    return pltpu.with_memory_space_constraint(v, pltpu.HBM)


def here(v):
    return pltpu.with_memory_space_constraint(v, pltpu.VMEM)


class Order:
    def __init__(self):
        self.last = ()


def call(body, grid, ins, in_specs, outs, out_specs, scratch=(), aliases=None, order=None, vmem=24):
    n_in, n_out = len(ins), len(outs)

    def kernel(*refs):
        after_in = n_in + len(order.last)
        body(*refs[:n_in], *refs[after_in : after_in + n_out], *refs[after_in + n_out + 1 :])

    *res, token = pl.pallas_call(
        kernel,
        grid=grid,
        in_specs=list(in_specs) + [anywhere()] * len(order.last),
        out_specs=list(out_specs) + [anywhere()],
        out_shape=list(outs) + [pltpu.HBM((8, 128), F32)],
        scratch_shapes=list(scratch),
        input_output_aliases=aliases or {},
        compiler_params=pltpu.CompilerParams(vmem_limit_bytes=vmem * MIB),
        cost_estimate=pl.CostEstimate(flops=COST, bytes_accessed=COST, transcendentals=0),
    )(*ins, *[in_hbm(v) for v in order.last])
    order.last = (token,)
    return res


def sds(shape, dtype):
    return jax.ShapeDtypeStruct(shape, dtype)


def normed(v):
    centred = v - jnp.mean(v, axis=-1, keepdims=True)
    inverse = lax.rsqrt(jnp.mean(centred * centred, axis=-1, keepdims=True) + EPS)
    return centred * inverse, inverse


def norm_back(e, n, inverse, gain):
    eg = e * gain
    return inverse * (
        eg - jnp.mean(eg, axis=-1, keepdims=True) - n * jnp.mean(eg * n, axis=-1, keepdims=True)
    )


def colsum(v):
    return jnp.sum(v, axis=0, keepdims=True)


def in_vmem():
    return pl.BlockSpec(memory_space=pltpu.VMEM)


BITS = {"x": 0, "y": 1, "a": 2, "b": 3}
HALVING = ("x", "y", "a", "b")


hbm = pltpu.HBM
vmem = pltpu.VMEM


class Links:
    def __init__(self, n_dp, n_t):
        self.n_dp, self.n_t = n_dp, n_t
        self.extra = tuple(range(4, n_dp.bit_length() - 1))

    def swap(self, v, dims):
        pairs = [
            (d * self.n_t + t, (d ^ (1 << BITS.get(dims[t % 2], dims[t % 2]))) * self.n_t + t)
            for d in range(self.n_dp)
            for t in range(self.n_t)
        ]
        return lax.ppermute(v, ("dp", "tensor"), pairs)

    def table(self):
        d, t = lax.axis_index("dp"), lax.axis_index("tensor") % 2
        return [
            ((d >> jnp.where(t == 0, BITS[v], BITS[w])) & 1).reshape(1) for v in HALVING for w in HALVING
        ]

    def place(self, dims):
        return HALVING.index(dims[0]) * 4 + HALVING.index(dims[1])


def add_split(keep, got, side_of, order):
    n, width = keep.shape
    h = n // 2

    def body(b_ref, k_ref, r_ref, ko_ref, so_ref):
        side = b_ref[0]
        mine = pl.ds(pl.multiple_of(side * h, 8), h)
        rest = pl.ds(pl.multiple_of((1 - side) * h, 8), h)
        so_ref[...] = k_ref[rest, :] + r_ref[rest, :]
        ko_ref[...] = k_ref[mine, :] + r_ref[mine, :]

    return call(
        body, (), [side_of, keep, got], [smem(), in_vmem(), in_vmem()],
        [sds((h, width), F32)] * 2, [in_vmem()] * 2, order=order, vmem=5,
    )


def add(keep, got, order):
    def body(k_ref, r_ref, o_ref):
        o_ref[...] = k_ref[...] + r_ref[...]

    return call(
        body, (), [keep, got], [in_vmem()] * 2, [sds(keep.shape, F32)], [in_vmem()], order=order, vmem=5
    )[0]


def join(mine, got, side_of, order):
    n, width = mine.shape

    def body(b_ref, m_ref, r_ref, o_ref):
        side = b_ref[0]
        o_ref[pl.ds(pl.multiple_of(side * n, 8), n), :] = m_ref[...]
        o_ref[pl.ds(pl.multiple_of((1 - side) * n, 8), n), :] = r_ref[...]

    return call(
        body, (), [side_of, mine, got], [smem(), in_vmem(), in_vmem()],
        [sds((2 * n, width), F32)], [in_vmem()], order=order, vmem=5,
    )[0]


class Piece:
    def __init__(self, links, sides, dims, keep, send, finish):
        self.links, self.sides, self.finish = links, sides, finish
        *halving, last = zip(*dims)
        whole = [last] + [(e, e) for e in links.extra]
        self.stages = (
            [(d, "half") for d in halving] + [(d, "whole") for d in whole] + [(d, "back") for d in halving[::-1]]
        )
        self.at = 0
        self.keep = keep
        self.got = links.swap(send, halving[0])

    def step(self, order):
        dim, kind = self.stages[self.at]
        self.at += 1
        if self.at == len(self.stages):
            self.finish(self.keep, self.got, order)
            return
        following, next_kind = self.stages[self.at]
        if kind == "back":
            self.keep = send = join(self.keep, self.got, self.sides[self.links.place(dim)], order)
        elif next_kind == "half":
            self.keep, send = add_split(self.keep, self.got, self.sides[self.links.place(following)], order)
        else:
            self.keep = send = add(self.keep, self.got, order)
        self.got = self.links.swap(send, following)


def on_device(
    links,
    plan,
    tokens,
    cotangent,
    caption_lengths,
    item_counts,
    w_qkv,
    qv_bias,
    w_out,
    out_bias,
    w_up,
    up_bias,
    w_down,
    down_bias,
    ln_gains,
    ln_biases,
):
    order = Order()
    sides = links.table()
    first = [sides[links.place((v[0][0], v[1][0]))] for v in plan["dims"]]
    items, seq, D = tokens.shape
    W = w_qkv.shape[2]
    FL = w_up.shape[1]
    pairs = W // 128
    heads = W // HEAD_DIM
    SP = -(-seq // 64) * 64
    R = items * SP
    IB = 2
    BR = IB * SP
    steps = items // IB
    scale = HEAD_DIM ** (-0.5)

    wq = jnp.transpose(w_qkv, (1, 0, 2))
    out_b = out_bias.reshape(1, D)
    down_b = down_bias.reshape(1, D)
    up_b = up_bias.reshape(1, FL)
    by_token = (1, 0, 2)
    state = {}
    pieces = {}
    up_sums = []
    swap = [(0, 1), (1, 0)]

    def other(v):
        return lax.ppermute(v, "tensor", swap)

    rowD = pl.BlockSpec((BR, D), lambda t: (t, 0))
    rowW = pl.BlockSpec((BR, W), lambda t: (t, 0))
    row3 = pl.BlockSpec((BR, 3 * W), lambda t: (t, 0))

    def release(arrays, space):
        n = len(arrays)
        return call(
            lambda *refs: None,
            (),
            [pltpu.with_memory_space_constraint(v, space) for v in arrays],
            [anywhere()] * n,
            [space(v.shape, v.dtype) for v in arrays],
            [anywhere()] * n,
            aliases={i: i for i in range(n)},
            order=order,
            vmem=4,
        )

    def dc_send():
        state["dc"] = release([state["dc"]], vmem)[0]
        state["dc_got"] = other(state["dc"])

    def da_send():
        state["da"] = release([state["da"]], vmem)[0]
        state["da_got"] = other(state["da"])

    def y_send():
        state["y"] = release([state["y"]], vmem)[0]
        state["y_got"] = other(state["y"])

    def spread(name, source, masked, parts):
        size = seq // parts

        def body(cnt_ref, *rest):
            t_ref, o_ref, sum_ref, xs, *more = rest[len(sides) :]
            rows = size * items
            if parts > 1:
                held, sems = more
                copies = [
                    pltpu.make_async_copy(t_ref.at[pl.ds(c * size, size)], held.at[c], sems.at[c]) for c in range(parts)
                ]
                for copy in copies:
                    copy.start()
            for c in range(parts):
                if parts > 1:
                    copies[c].wait()
                for k in range(D // 128):
                    cols = pl.ds(k * 128, 128)
                    v = held[c, :, :, cols] if parts > 1 else t_ref[:, :, cols]
                    xs[k, pl.ds(c * rows, rows), :] = v.astype(F32).reshape(rows, 128)
            for k in range(D // 128):
                cols = pl.ds(k * 128, 128)
                xs[k, pl.ds(seq * items, (SP - seq) * items), :] = jnp.zeros(((SP - seq) * items, 128), F32)
                total = jnp.zeros((1, 128), F32)
                for i in range(items):
                    v = xs[k, pl.ds(i, SP, stride=items), :]
                    if masked:
                        v = jnp.where(i < cnt_ref[0], v, 0.0)
                        total = total + colsum(v)
                    o_ref[pl.ds(i * SP, SP), cols] = v.astype(BF16)
                sum_ref[:, cols] = total

        by_tokens = jnp.transpose(source, by_token)
        scratch = [pltpu.VMEM((D // 128, SP * items, 128), F32)]
        if parts > 1:
            scratch += [pltpu.VMEM((parts, size, items, D), BF16), pltpu.SemaphoreType.DMA((parts,))]
        state[name], state[name + "_sum"] = call(
            body,
            (),
            [item_counts, *sides, in_hbm(by_tokens) if parts > 1 else by_tokens],
            [smem()] * (1 + len(sides)) + [anywhere() if parts > 1 else in_vmem()],
            [vmem((R, D), BF16), sds((1, D), F32)],
            [in_vmem()] * 2,
            scratch,
            order=order,
            vmem=12,
        )

    IH = items // 2
    RH = R // 2

    def attn_fwd(half):
        off = half * RH
        names = ("a", "qkv", "pr", "ctx", "x_kept")

        def body(len_ref, x_ref, wq_ref, qvb_ref, g_ref, b_ref, wo_ref, *rest):
            part_ref, a_out, qkv_out, pr_out, ctx_out, x_out, a_ref, qkv_ref, pr_ref, ctx_ref, sems = rest[-11:]
            mine = pl.ds(off, RH)
            copies = []

            def copy_out(source, target):
                copy = pltpu.make_async_copy(source, target, sems.at[len(copies)])
                copy.start()
                copies.append(copy)

            copy_out(x_ref.at[mine], x_out.at[mine])
            n, _ = normed(x_ref[mine, :].astype(F32))
            a = (n * g_ref[0:1] + b_ref[0:1]).astype(BF16)
            a_ref[...] = a
            copy_out(a_ref, a_out.at[mine])
            for c in range(3):
                cols = pl.ds(c * W, W)
                v = mm(a, wq_ref[c])
                if c != 1:
                    v = v + qvb_ref[c // 2 : c // 2 + 1]
                qkv_ref[:, cols] = v.astype(BF16)
            copy_out(qkv_ref, qkv_out.at[mine])
            lane = lax.broadcasted_iota(jnp.int32, (SP, 128), 1)
            key_at = lax.broadcasted_iota(jnp.int32, (SP, SP), 0)
            zero = jnp.zeros((SP, 128), BF16)
            for i in range(IH):
                valid = key_at < PATCHES + 1 + len_ref[half * IH + i]
                rows = pl.ds(i * SP, SP)
                for j in range(pairs):
                    q = qkv_ref[rows, pl.ds(j * 128, 128)] * jnp.asarray(scale, BF16)
                    k = qkv_ref[rows, pl.ds(W + j * 128, 128)]
                    v = qkv_ref[rows, pl.ds(2 * W + j * 128, 128)]
                    ctx = None
                    for s in range(2):
                        side = (lane < 64) if s == 0 else (lane >= 64)
                        st = mm(k, jnp.where(side, q, zero), 1, 1)
                        st = jnp.where(valid, st, -1e30)
                        e = jnp.exp(st - jnp.max(st, axis=0, keepdims=True))
                        pr = (e * (1.0 / jnp.sum(e, axis=0, keepdims=True))).astype(BF16)
                        pr_ref[i, 2 * j + s] = pr
                        c = mm(pr, jnp.where(side, v, zero), 0, 0)
                        ctx = c if ctx is None else ctx + c
                    ctx_ref[rows, pl.ds(j * 128, 128)] = ctx.astype(BF16)
                copy_out(pr_ref.at[i], pr_out.at[half * IH + i])
            copy_out(ctx_ref, ctx_out.at[mine])
            part_ref[...] = mm(ctx_ref[...], wo_ref[...])
            for copy in copies:
                copy.wait()

        ins = [in_hbm(caption_lengths), here(state["x"]), wq, in_hbm(qv_bias), in_hbm(ln_gains), in_hbm(ln_biases), w_out]
        specs = [smem()] + [in_vmem()] * 6
        outs = [
            vmem((RH, D), F32),
            hbm((R, D), BF16),
            hbm((R, 3 * W), BF16),
            hbm((items, heads, SP, SP), BF16),
            hbm((R, W), BF16),
            hbm((R, D), BF16),
        ]
        aliases = {}
        if half:
            aliases = {len(ins) + n: 1 + n for n in range(5)}
            ins += [in_hbm(state[v]) for v in names]
            specs += [anywhere()] * 5
        part, *kept = call(
            body,
            (),
            ins,
            specs,
            outs,
            [in_vmem()] + [anywhere()] * 5,
            [
                pltpu.VMEM((RH, D), BF16),
                pltpu.VMEM((RH, 3 * W), BF16),
                pltpu.VMEM((IH, heads, SP, SP), BF16),
                pltpu.VMEM((RH, W), BF16),
                pltpu.SemaphoreType.DMA((4 + IH,)),
            ],
            aliases,
            order=order,
            vmem=16,
        )
        state.update(zip(names, kept))
        return part

    spread("x", tokens, False, 5 if seq % 5 == 0 else 1)
    parts, got = [], []
    for half in range(2):
        part = attn_fwd(half)
        parts.append(part)
        got.append(other(part))

    def second(half):
        def body(x_ref, p_ref, r_ref, ob_ref, g_ref, b_ref, *rest):
            h_ref, c_ref, ct_ref = rest[-3:]
            h = x_ref[...].astype(F32) + (p_ref[...] + r_ref[...]) + ob_ref[...]
            h_ref[...] = h.astype(BF16)
            n, _ = normed(h)
            c = (n * g_ref[1:2] + b_ref[1:2]).astype(BF16)
            c_ref[...] = c
            ct_ref[...] = c.T

        off = half * (steps // 2)
        row = lambda t: (t + off, 0)
        ins = [state["x"], parts[half], got[half], out_b, ln_gains, ln_biases]
        specs = [pl.BlockSpec((BR, D), row), rowD, rowD, in_vmem(), in_vmem(), in_vmem()]
        outs = [vmem((R, D), BF16), vmem((R, D), BF16), vmem((D, R), BF16)]
        out_specs = [
            pl.BlockSpec((BR, D), row),
            pl.BlockSpec((BR, D), row),
            pl.BlockSpec((D, BR), lambda t: (0, t + off)),
        ]
        names = ("h", "c", "ct")
        aliases = {}
        if half:
            aliases = {len(ins) + n: n for n in range(3)}
            ins += [here(state["h"]), here(state["c"]), here(state["ct"])]
            specs += [anywhere()] * 3
        kept = call(
            body, (steps // 2,), ins, specs, outs, out_specs, (), aliases, order=order, vmem=11
        )
        state.update(zip(names, kept))

    second(0)
    spread("dy", cotangent, True, 1)
    second(1)

    sizes = [128 * v for v in plan["units"]]
    chunks = len(sizes)
    starts = [sum(sizes[:f]) for f in range(chunks)]
    SB = 256
    DH = D // 2
    HL = FL // 2
    blocks = DH // 128

    def ffn(f):
        HU = sizes[f]
        FC = 2 * HU

        def body(p_ref, c_ref, ct_ref, dy_ref, wu_ref, ub_ref, wd_ref, keep_ref, send_ref, sum_ref, r_ref, du_ref, acc):
            p = p_ref[0]
            units = [pl.ds(starts[f] + side * HL, HU) for side in range(2)]
            wu = jnp.concatenate([wu_ref[:, v] for v in units], axis=1)
            wd = jnp.concatenate([wd_ref[v, :] for v in units], axis=0)
            ub = jnp.concatenate([ub_ref[:, v] for v in units], axis=1)
            total = jnp.zeros((1, FC), F32)
            for s in range(R // SB):
                rows = pl.ds(s * SB, SB)
                u = mm(c_ref[rows, :], wu) + ub
                dr = mm(dy_ref[rows, :], wd, 1, 1)
                below = 0.5 + 0.5 * lax.erf(u * (0.5**0.5))
                density = jnp.exp(-0.5 * u * u) * 0.3989422804014327
                r_ref[rows, :] = (u * below).astype(BF16)
                du = (dr * (below + u * density)).astype(BF16)
                du_ref[rows, :] = du
                total = total + colsum(du.astype(F32))
            sum_ref[...] = total
            gd = mm(r_ref[...], dy_ref[...], 0, 0)
            for half in range(2):
                acc[half, pl.ds(0, HU), :] = gd[half * HU : (half + 1) * HU]
            gu = mm(ct_ref[...], du_ref[...])
            for half in range(2):
                for j in range(HU // 128):
                    for b in range(blocks):
                        for side in range(2):
                            acc[half, pl.ds(HU + j * 128, 128), pl.ds((2 * b + side) * 128, 128)] = gu[
                                half * DH + b * 128 : half * DH + (b + 1) * 128,
                                side * HU + j * 128 : side * HU + (j + 1) * 128,
                            ]
            keep_ref[...] = acc[p]
            send_ref[...] = acc[1 - p]

        keep, send, total, state["r", f], state["du", f] = call(
            body,
            (),
            [first[f], here(state["c"]), here(state["ct"]), here(state["dy"]), w_up, up_b, w_down],
            [smem()] + [in_vmem()] * 6,
            [
                vmem((FC, D), F32),
                vmem((FC, D), F32),
                sds((1, FC), F32),
                vmem((R, FC), BF16),
                vmem((R, FC), BF16),
            ],
            [in_vmem()] * 5,
            [pltpu.VMEM((2, FC, D), F32)],
            order=order,
            vmem=10,
        )
        up_sums.append(total)

        def finish(mine, got, order):
            def body(p_ref, m_ref, g_ref, *rest):
                gd_ref, gu_ref = rest[-2:]
                own = pl.program_id(0) == p_ref[0]

                def write(ref, side):
                    gd_ref[...] = ref[pl.ds(0, HU), :]
                    for j in range(HU // 128):
                        for b in range(blocks):
                            gu_ref[pl.ds(b * 128, 128), pl.ds(j * 128, 128)] = ref[
                                pl.ds(HU + j * 128, 128), pl.ds((2 * b + side) * 128, 128)
                            ]

                for side in range(2):
                    this = pl.program_id(1) == side

                    @pl.when(own & this)
                    def _(side=side):
                        write(m_ref, side)

                    @pl.when(jnp.logical_not(own) & this)
                    def _(side=side):
                        write(g_ref, side)

            ins, specs, aliases = [first[f], mine, got], [smem(), in_vmem(), in_vmem()], {}
            if "gd" in state:
                aliases = {3: 0, 4: 1}
                ins += [in_hbm(state["gd"]), in_hbm(state["gu"])]
                specs += [anywhere()] * 2
            state["gd"], state["gu"] = call(
                body,
                (2, 2),
                ins,
                specs,
                [hbm((FL, D), F32), hbm((D, FL), F32)],
                [
                    pl.BlockSpec((HU, D), lambda t, s: ((t * HL + starts[f]) // HU, 0)),
                    pl.BlockSpec((DH, HU), lambda t, s: (t, (s * HL + starts[f]) // HU)),
                ],
                aliases=aliases,
                order=order,
                vmem=10,
            )

        pieces[f] = Piece(links, sides, plan["dims"][f], keep, send, finish)

    def in_order(refs):
        return jnp.concatenate(
            [ref[:, pl.ds(side * hu, hu)] for side in range(2) for ref, hu in zip(refs, sizes)], axis=1
        )

    def dc():
        def body(*refs):
            refs[-1][...] = mm(in_order(refs[:-2]), refs[-2][...], 1, 1)

        rowF = [pl.BlockSpec((BR, 2 * hu), lambda t: (t, 0)) for hu in sizes]
        (state["dc"],) = call(
            body,
            (steps,),
            [here(state["du", f]) for f in range(chunks)] + [w_up],
            rowF + [in_vmem()],
            [vmem((R, D), F32)],
            [rowD],
            order=order,
            vmem=6,
        )

    def y():
        def body(*refs):
            refs[-1][...] = mm(in_order(refs[:-2]), refs[-2][...])

        rowF = [pl.BlockSpec((BR, 2 * hu), lambda t: (t, 0)) for hu in sizes]
        (state["y"],) = call(
            body,
            (steps,),
            [here(state["r", f]) for f in range(chunks)] + [w_down],
            rowF + [in_vmem()],
            [vmem((R, D), F32)],
            [rowD],
            order=order,
            vmem=8,
        )

    def back2():
        def body(h_ref, dy_ref, ctx_ref, wo_ref, g_ref, e0_ref, e1_ref, dh_ref, dctx_ref, go_ref, sum_ref):
            step = pl.program_id(0)
            e = e0_ref[...] + e1_ref[...]
            n, inverse = normed(h_ref[...].astype(F32))
            dh = dy_ref[...].astype(F32) + norm_back(e, n, inverse, g_ref[1:2])
            dhr = dh.astype(BF16)
            dh_ref[...] = dhr
            dctx_ref[...] = mm(dhr, wo_ref[...], 1, 1).astype(BF16)
            sum_ref[0, 0:1] = colsum(e * n)
            sum_ref[0, 1:2] = colsum(e)
            sum_ref[0, 2:3] = colsum(dhr.astype(F32))
            go = mm(ctx_ref[...], dhr, 0, 0)

            @pl.when(step == 0)
            def _():
                go_ref[...] = go

            @pl.when(step > 0)
            def _():
                go_ref[...] += go

        state["dh"], state["dctx"], state["go"], state["back2"] = call(
            body,
            (steps,),
            [here(state["h"]), here(state["dy"]), in_hbm(state["ctx"]), w_out, ln_gains]
            + [here(state["dc"]), here(state["dc_got"])],
            [rowD, rowD, rowW, in_vmem(), in_vmem(), rowD, rowD],
            [hbm((R, D), BF16), vmem((R, W), BF16), sds((W, D), F32), sds((steps, 3, D), F32)],
            [rowD, rowW, whole((W, D)), pl.BlockSpec((1, 3, D), lambda t: (t, 0, 0))],
            order=order,
            vmem=10,
        )

    def attn_back(half):
        def body(pr_ref, qkv_ref, dctx_ref, *rest):
            dqkv_ref, sum_ref = rest[-2:]
            lane = lax.broadcasted_iota(jnp.int32, (SP, 128), 1)
            zero = jnp.zeros((SP, 128), BF16)
            for i in range(IB):
                rows = pl.ds(i * SP, SP)
                for j in range(pairs):
                    q = qkv_ref[rows, pl.ds(j * 128, 128)] * jnp.asarray(scale, BF16)
                    k = qkv_ref[rows, pl.ds(W + j * 128, 128)]
                    v = qkv_ref[rows, pl.ds(2 * W + j * 128, 128)]
                    dctx = dctx_ref[rows, pl.ds(j * 128, 128)]
                    dq = dk = dv = None
                    for s in range(2):
                        mine = (lane < 64) if s == 0 else (lane >= 64)
                        pr = pr_ref[i, 2 * j + s]
                        dc = jnp.where(mine, dctx, zero)
                        dv_h = mm(pr, dc)
                        dp = mm(v, dc, 1, 1)
                        p = pr.astype(F32)
                        pdp = p * dp
                        ds = (pdp - p * jnp.sum(pdp, axis=0, keepdims=True)).astype(BF16)
                        dk_h = mm(ds, jnp.where(mine, q, zero))
                        dq_h = mm(ds, jnp.where(mine, k, zero), 0, 0)
                        dq = dq_h if dq is None else dq + dq_h
                        dk = dk_h if dk is None else dk + dk_h
                        dv = dv_h if dv is None else dv + dv_h
                    dqkv_ref[rows, pl.ds(j * 128, 128)] = (dq * scale).astype(BF16)
                    dqkv_ref[rows, pl.ds(W + j * 128, 128)] = dk.astype(BF16)
                    dqkv_ref[rows, pl.ds(2 * W + j * 128, 128)] = dv.astype(BF16)
            sum_ref[0] = colsum(dqkv_ref[...].astype(F32))

        off = half * (steps // 2)
        ins = [in_hbm(state["pr"]), in_hbm(state["qkv"]), here(state["dctx"])]
        specs = [
            pl.BlockSpec((IB, heads, SP, SP), lambda t: (t + off, 0, 0, 0)),
            pl.BlockSpec((BR, 3 * W), lambda t: (t + off, 0)),
            pl.BlockSpec((BR, W), lambda t: (t + off, 0)),
        ]
        aliases = {}
        if half:
            aliases = {3: 0, 4: 1}
            ins += [here(state["dqkv"]), here(state["qkv_sums"])]
            specs += [anywhere()] * 2
        state["dqkv"], state["qkv_sums"] = call(
            body,
            (steps // 2,),
            ins,
            specs,
            [vmem((R, 3 * W), BF16), vmem((steps, 1, 3 * W), F32)],
            [
                pl.BlockSpec((BR, 3 * W), lambda t: (t + off, 0)),
                pl.BlockSpec((1, 1, 3 * W), lambda t: (t + off, 0, 0)),
            ],
            aliases=aliases,
            order=order,
            vmem=8,
        )

    def da():
        def body(d_ref, w_ref, o_ref):
            v = None
            for c in range(3):
                term = mm(d_ref[:, pl.ds(c * W, W)], w_ref[c], 1, 1)
                v = term if v is None else v + term
            o_ref[...] = v

        (state["da"],) = call(
            body,
            (steps,),
            [here(state["dqkv"]), wq],
            [row3, in_vmem()],
            [vmem((R, D), F32)],
            [rowD],
            order=order,
            vmem=6,
        )

    DQ, WH = DH // 2, W // 2

    def packed(v):
        return jnp.concatenate([v[:DQ], v[DQ:]], axis=1)

    def gqkv():
        def body(p_ref, p4_ref, a_ref, dqkv_ref, go_ref, k3_ref, s3_ref, k4_ref, s4_ref, at, tmp):
            step = pl.program_id(0)
            p = p_ref[0]
            p4 = p4_ref[0]

            @pl.when(step == 0)
            def _():
                at[...] = a_ref[...].T

            @pl.when(step < 3)
            def _():
                g = mm(at[...], dqkv_ref[...])
                tmp[0] = packed(g[:DH])
                tmp[1] = packed(g[DH:])

            @pl.when(step < 2)
            def _():
                k3_ref[...] = tmp[p]
                s3_ref[...] = tmp[1 - p]

            @pl.when(step == 2)
            def _():
                k4_ref[...] = tmp[p4]
                s4_ref[...] = tmp[1 - p4]

            @pl.when(step == 3)
            def _():
                k4_ref[...] = go_ref[pl.ds(pl.multiple_of(p4 * WH, 8), WH), :]
                s4_ref[...] = go_ref[pl.ds(pl.multiple_of((1 - p4) * WH, 8), WH), :]

        first_half = pl.BlockSpec((DQ, D), lambda t: (jnp.minimum(t, 1), 0))
        second_half = pl.BlockSpec((DQ, D), lambda t: (jnp.maximum(t - 2, 0), 0))
        k3, s3, k4, s4 = call(
            body,
            (4,),
            [first[chunks], first[chunks + 1], state["a"], here(state["dqkv"]), state["go"]],
            [smem(), smem(), in_vmem(), pl.BlockSpec((R, W), lambda t: (0, jnp.minimum(t, 2))), in_vmem()],
            [vmem((DH, D), F32)] * 4,
            [first_half, first_half, second_half, second_half],
            [pltpu.VMEM((D, R), BF16), pltpu.VMEM((2, DQ, D), F32)],
            order=order,
            vmem=10,
        )

        def finish3(mine, got, order):
            def body(p_ref, m_ref, g_ref, *rest):
                o_ref = rest[-1]
                own = pl.program_id(0) == p_ref[0]

                def write(ref):
                    for c in range(2):
                        for b in range(2):
                            o_ref[c, pl.ds(b * DQ, DQ), :] = ref[pl.ds(c * DQ, DQ), pl.ds(b * W, W)]

                @pl.when(own)
                def _():
                    write(m_ref)

                @pl.when(jnp.logical_not(own))
                def _():
                    write(g_ref)

            ins, specs, aliases = [first[chunks], mine, got], [smem(), in_vmem(), in_vmem()], {}
            if "gqkv" in state:
                aliases = {3: 0}
                ins += [in_hbm(state["gqkv"])]
                specs += [anywhere()]
            (state["gqkv"],) = call(
                body, (2,), ins, specs, [hbm((3, D, W), F32)],
                [pl.BlockSpec((2, DH, W), lambda t: (0, t, 0))], aliases=aliases, order=order, vmem=10,
            )

        def finish4(mine, got, order):
            def body(p_ref, m_ref, g_ref, *rest):
                o_ref, go_ref = rest[-2:]
                own = pl.program_id(0) == p_ref[0]

                def write(ref):
                    for b in range(2):
                        o_ref[0, pl.ds(b * DQ, DQ), :] = ref[pl.ds(0, DQ), pl.ds(b * W, W)]
                    go_ref[...] = ref[pl.ds(DQ, WH), :]

                @pl.when(own)
                def _():
                    write(m_ref)

                @pl.when(jnp.logical_not(own))
                def _():
                    write(g_ref)

            ins, specs, aliases = [first[chunks + 1], mine, got], [smem(), in_vmem(), in_vmem()], {}
            if "gqkv" in state:
                aliases = {3: 0}
                ins += [in_hbm(state["gqkv"])]
                specs += [anywhere()]
            state["gqkv"], state["grad_out"] = call(
                body, (2,), ins, specs, [hbm((3, D, W), F32), hbm((W, D), F32)],
                [pl.BlockSpec((1, DH, W), lambda t: (2, t, 0)), pl.BlockSpec((WH, D), lambda t: (t, 0))],
                aliases=aliases, order=order, vmem=10,
            )

        def start():
            send3, send4 = release([s3, s4], vmem)
            pieces[chunks] = Piece(links, sides, plan["dims"][chunks], k3, send3, finish3)
            pieces[chunks + 1] = Piece(links, sides, plan["dims"][chunks + 1], k4, send4, finish4)

        state["qkv_send"] = start

    def gather_rows(ys, o_ref):
        @pl.when(pl.program_id(0) == steps - 1)
        def _():
            for k in range(D // 128):
                v = ys[k, pl.ds(0, seq * items), :].reshape(seq, items, 128)
                o_ref[:, :, pl.ds(k * 128, 128)] = v.astype(BF16)

    def put_rows(ys, v):
        step = pl.program_id(0)
        for j in range(steps):

            @pl.when(step == j)
            def _(j=j):
                for i in range(IB):
                    for k in range(D // 128):
                        ys[k, pl.ds(j * IB + i, SP, stride=items), :] = v[
                            i * SP : (i + 1) * SP, k * 128 : (k + 1) * 128
                        ]

    def back1():
        def body(x_ref, dh_ref, g_ref, e0_ref, e1_ref, o_ref, sum_ref, ys):
            e = e0_ref[...] + e1_ref[...]
            n, inverse = normed(x_ref[...].astype(F32))
            dx = dh_ref[...].astype(F32) + norm_back(e, n, inverse, g_ref[0:1])
            put_rows(ys, dx)
            sum_ref[0, 0:1] = colsum(e * n)
            sum_ref[0, 1:2] = colsum(e)
            gather_rows(ys, o_ref)

        state["grad_tokens"], state["back1"] = call(
            body,
            (steps,),
            [in_hbm(state["x_kept"]), in_hbm(state["dh"]), ln_gains, here(state["da"]), here(state["da_got"])],
            [rowD, rowD, in_vmem(), rowD, rowD],
            [hbm((seq, items, D), BF16), sds((steps, 2, D), F32)],
            [whole((seq, items, D)), pl.BlockSpec((1, 2, D), lambda t: (t, 0, 0))],
            [pltpu.VMEM((D // 128, SP * items, 128), F32)],
            order=order,
            vmem=17,
        )

    def out():
        def body(cnt_ref, h_ref, p_ref, r_ref, b_ref, o_ref, ys):
            step = pl.program_id(0)
            v = h_ref[...].astype(F32) + (p_ref[...] + r_ref[...]) + b_ref[...]
            item = step * IB + lax.broadcasted_iota(jnp.int32, (BR, D), 0) // SP
            put_rows(ys, jnp.where(item < cnt_ref[0], v, 0.0))
            gather_rows(ys, o_ref)

        (state["output"],) = call(
            body,
            (steps,),
            [item_counts, here(state["h"]), here(state["y"]), here(state["y_got"]), down_b],
            [smem(), rowD, rowD, rowD, in_vmem()],
            [hbm((seq, items, D), BF16)],
            [whole((seq, items, D))],
            [pltpu.VMEM((D // 128, SP * items, 128), F32)],
            order=order,
            vmem=17,
        )

    SR = 16

    def gather():
        def body(q_ref, b2_ref, dy_ref, b1_ref, *rest):
            ups, o_ref = rest[:-1], rest[-1]
            o_ref[...] = jnp.zeros((SR, D), F32)
            qs = jnp.sum(q_ref[...], axis=0)
            o_ref[0:1, pl.ds(0, W)] = qs[:, :W]
            o_ref[0:1, pl.ds(W, W)] = qs[:, 2 * W :]
            o_ref[1:4, :] = jnp.sum(b2_ref[...], axis=0)
            for up, at, hu in zip(ups, starts, sizes):
                for side in range(2):
                    o_ref[4 + side : 5 + side, pl.ds(at, hu)] = up[:, pl.ds(side * hu, hu)]
            o_ref[6:7, :] = dy_ref[...]
            o_ref[7:9, :] = jnp.sum(b1_ref[...], axis=0)

        ins = [state["qkv_sums"], state["back2"], state["dy_sum"], state["back1"]] + up_sums
        state["small"] = call(
            body, (), ins, [in_vmem()] * len(ins), [sds((SR, D), F32)], [in_vmem()], order=order, vmem=8
        )[0]
        state["small_dims"] = [("x", "y"), ("y", "x"), ("a", "a"), ("b", "b")] + [(e, e) for e in links.extra]
        state["small_got"] = links.swap(state["small"], state["small_dims"].pop(0))

    def small():
        if state["small_dims"]:
            state["small"] = add(state["small"], state["small_got"], order)
            state["small_got"] = links.swap(state["small"], state["small_dims"].pop(0))
            return

        def body(a_ref, b_ref, qb_ref, ob_ref, ub_ref, db_ref, gg_ref, gb_ref):
            s = a_ref[...] + b_ref[...]
            qb_ref[0:1, :] = s[0:1, :W]
            qb_ref[1:2, :] = s[0:1, W:]
            gg_ref[1:2, :] = s[1:2]
            gb_ref[1:2, :] = s[2:3]
            ob_ref[...] = s[3]
            ub_ref[pl.ds(0, D)] = s[4]
            ub_ref[pl.ds(D, D)] = s[5]
            db_ref[...] = s[6]
            gg_ref[0:1, :] = s[7:8]
            gb_ref[0:1, :] = s[8:9]

        shapes = [(2, W), (D,), (FL,), (D,), (2, D), (2, D)]
        state["small_outs"] = call(
            body, (), [state["small"], state["small_got"]], [in_vmem()] * 2,
            [sds(v, F32) for v in shapes], [in_vmem()] * len(shapes), order=order, vmem=8,
        )

    jobs = {
        "dc": dc, "y": y, "back2": back2, "attn": lambda: attn_back(0), "attn2": lambda: attn_back(1), "gqkv": gqkv, "da": da, "back1": back1, "out": out,
        "gather": gather, "small": small, "dc_send": dc_send, "da_send": da_send, "y_send": y_send,
        "qkv_send": lambda: state["qkv_send"](),
    }
    for job in plan["order"]:
        if job in jobs:
            jobs[job]()
        elif job.startswith("F"):
            ffn(int(job[1:]))
        else:
            pieces[int(job)].step(order)
    for piece in pieces.values():
        while piece.at < len(piece.stages):
            piece.step(order)
    while "small_outs" not in state:
        small()
    qb, ob, ub, db, gg, gb = state["small_outs"]
    return (
        jnp.transpose(state["output"], by_token),
        jnp.transpose(state["grad_tokens"], by_token),
        jnp.transpose(state["gqkv"], (1, 0, 2)),
        qb,
        state["grad_out"],
        ob,
        state["gu"],
        ub,
        state["gd"],
        db,
        gg,
        gb,
    )


PLAN = {
    "units": (1, 1, 2, 2),
    "dims": (("xyab", "yxab"), ("xyba", "yxba"), ("yxab", "xyab"), ("ayxb", "axyb"), ("yxab", "xyab"), ("yxab", "xyab")),
    "order": (
        "F0", "F1", "F2", "F3", "dc", "0", "1", "dc_send", "back2", "attn", "2", "attn2", "gqkv", "0", "1",
        "qkv_send", "2", "3", "da", "2", "da_send", "1", "5", "3", "y", "0", "2", "1", "0", "5", "4", "2", "3",
        "y_send", "back1", "5", "2", "4", "out", "3", "0", "4", "gather", "5", "3", "0", "4", "small", "5", "5",
        "3", "4", "2", "small", "1", "1", "0", "4", "5", "3", "small", "1", "small", "4",
    ),
}


def solution(mesh):
    links = Links(mesh.shape["dp"], mesh.shape["tensor"])

    def layer(*arrays):
        return on_device(links, PLAN, *arrays)

    return jax.shard_map(
        layer,
        mesh=mesh,
        in_specs=(
            P("dp", None, None),
            P("dp", None, None),
            P("dp"),
            P("dp"),
            P(None, None, "tensor"),
            P(None, "tensor"),
            P("tensor", None),
            P(),
            P(None, "tensor"),
            P("tensor"),
            P("tensor", None),
            P(),
            P(),
            P(),
        ),
        out_specs=(
            P("dp", None, None),
            P("dp", None, None),
            P(None, None, "tensor"),
            P(None, "tensor"),
            P("tensor", None),
            P(),
            P(None, "tensor"),
            P("tensor"),
            P("tensor", None),
            P(),
            P(),
            P(),
        ),
        check_vma=False,
    )
```
